512 devices in a mesh: gx: 32 (over x_hi, z, core), gy: 16 (over y, x_lo).
Axes of the slice: x: 4 (x_hi: 2, x_lo: 2; x = x_hi * 2 + x_lo), y: 8, z: 8, core: 2. Of those that a mesh axis runs over, the one named last changes fastest.
Arguments:
- voltages: bfloat16 [2, 2048, 1024, 128], P(None, 'gx', 'gy'), may hold values from -6 to 6
- beam_grid: int32 [1024, 2], replicated, may hold values from 0 to 255
- feed_pos: int32 [2048, 2], replicated, may hold values from 0 to 255
- rfi_mask: int32 [8, 16384], P(None, ('gy', 'gx')), may hold values 0 or 1
Outputs:
- power: bfloat16 [1024, 8, 16384], P(('gx', 'gy'))
- sk_sums: float32 [2, 1024, 16384], P(None, ('gx', 'gy'))
The draws below stay inside these ranges and needn't reach their ends.
All inputs are finite; a program needn't handle non-finite values. No bound on the sum of `rfi_mask` on one device may be relied on, other than what follows from the above.
Results may differ from the reference program's by a relative error of at most 0.0056.
Values may be sent and summed in bfloat16 or wider, within the bound.
No kernel may reach another device: no remote copies, remote signals or barrier semaphores. Data moves between devices by JAX's collectives and lax.ppermute only.
A program may use at most 64 MiB of HBM per device.

```python
import math
import jax
import jax.numpy as jnp
from jax import lax

FEEDS = 2048
BEAMS = 1024
UPCHAN = 16
TOUT = 8
TIME = 128
CHANNELS = 1024
FREQS = 16384


def plant(entries, own_key, low, top_value):
    dims = entries.shape
    spot = [jax.random.randint(jax.random.fold_in(own_key, axis), (), 0, dims[axis]) for axis in range(len(dims))]
    entries = entries.at[tuple(spot)].set(low)
    longest = dims.index(max(dims))
    spot[longest] = (spot[longest] + 1) % dims[longest]
    return entries.at[tuple(spot)].set(top_value)


def level_of(own_key, dims, cuts, least, top_value):
    loudness = 1.0
    for position, parts in cuts:
        draws = jax.random.uniform(jax.random.fold_in(jax.random.fold_in(own_key, 6), position), (parts,), jnp.float32, least / len(cuts), top_value / len(cuts))
        loudness = loudness * jnp.repeat(jnp.exp(draws), dims[position] // parts).reshape((-1,) + (1,) * (len(dims) - 1 - position))
    return loudness


def bell_draw(stream_key, dims, spread, limit, cuts=(), held_as=jnp.bfloat16):
    level = level_of(stream_key, dims, cuts, -0.22, 0.18) if cuts else 1.0
    values = jax.random.normal(stream_key, dims, jnp.float32) * spread * level
    return jnp.minimum(jnp.maximum(values, -limit), limit).astype(held_as)


def setup_inputs(seed: int = 0) -> dict:
    streams_of = jax.random.split(jax.random.key(seed), 5)
    return {
        "voltages": bell_draw(streams_of[0], (2, FEEDS, CHANNELS, TIME), 1.0, 6.0, ((1, 32), (2, 16))),
        "beam_grid": plant(jax.random.randint(streams_of[1], (BEAMS, 2), 0, 256), jax.random.fold_in(streams_of[1], 1), 0, 255).astype(jnp.int32),
        "feed_pos": plant(jax.random.randint(streams_of[2], (FEEDS, 2), 0, 256), jax.random.fold_in(streams_of[2], 1), 0, 255).astype(jnp.int32),
        "rfi_mask": plant((jax.random.randint(streams_of[3], (TOUT, FREQS), 0, 8) < 7).astype(jnp.int32), jax.random.fold_in(streams_of[3], 1), 0, 1),
    }


def dft_tables(time_len, upchan):
    rows = jnp.arange(time_len, dtype=jnp.int32)[:, None]
    cols = jnp.arange(time_len, dtype=jnp.int32)[None, :]
    same = (rows // upchan == cols // upchan).astype(jnp.float32)
    turns = rows % upchan * (cols % upchan) % upchan
    angle = turns.astype(jnp.float32) * (2.0 * math.pi / upchan)
    scale = 1.0 / math.sqrt(upchan)
    return (jnp.cos(angle) * same * scale, jnp.sin(angle) * same * scale)

def grid_phase(beam_grid, feed_pos):
    return (beam_grid[:, 0:1] * feed_pos[None, :, 0] + beam_grid[:, 1:2] * feed_pos[None, :, 1]) % 4096

def steering(grid_base, chan, feeds):
    turns = grid_base * ((chan + 400) % 4096) % 4096
    angle = turns.astype(jnp.float32) * (2.0 * math.pi / 4096.0)
    scale = 1.0 / math.sqrt(feeds)
    return jnp.concatenate([jnp.cos(angle) * scale, -jnp.sin(angle) * scale], 0).astype(jnp.bfloat16)

def reference(voltages, beam_grid, feed_pos, rfi_mask):
    grid_base = grid_phase(beam_grid, feed_pos)
    cos_table, sin_table = dft_tables(TIME, UPCHAN)
    hig = lax.Precision.HIGHEST

    def one_channel(chan):
        stack = steering(grid_base, chan, FEEDS)
        piece = lax.dynamic_slice_in_dim(voltages, chan, 1, 2)[:, :, 0, :]
        first = jnp.dot(stack, piece[0], preferred_element_type=jnp.float32)
        second = jnp.dot(stack, piece[1], preferred_element_type=jnp.float32)
        real_part = first[:BEAMS] - second[BEAMS:]
        imag_part = second[:BEAMS] + first[BEAMS:]
        fine_real = jnp.dot(real_part, cos_table, precision=hig) + jnp.dot(imag_part, sin_table, precision=hig)
        fine_imag = jnp.dot(imag_part, cos_table, precision=hig) - jnp.dot(real_part, sin_table, precision=hig)
        intensity = (fine_real * fine_real + fine_imag * fine_imag).reshape(BEAMS, TOUT, UPCHAN)
        bandpass = lax.optimization_barrier(jnp.mean(intensity, axis=(0, 1))) + 1e-06
        flags = lax.dynamic_slice_in_dim(rfi_mask, chan * UPCHAN, UPCHAN, 1).astype(jnp.float32)
        return (intensity / bandpass[None, None, :] * flags[None, :, :]).astype(jnp.bfloat16)
    chans = jnp.arange(CHANNELS, dtype=jnp.int32)
    stacked = lax.map(one_channel, chans)
    power = stacked.transpose(1, 2, 0, 3).reshape(BEAMS, TOUT, FREQS)
    values = power.astype(jnp.float32)
    sk_sums = jnp.stack([lax.optimization_barrier(jnp.sum(values, axis=1)), lax.optimization_barrier(jnp.sum(values * values, axis=1))], 0)
    return (power, sk_sums)
```

```python
import math

import jax
import jax.numpy as jnp
import numpy as np
from jax import lax
from jax.experimental import pallas as pl
from jax.experimental.pallas import tpu as pltpu
from jax.sharding import PartitionSpec as P

FEEDS = 2048
BEAMS = 1024
UPCHAN = 16
TOUT = 8
TIME = 128
F32 = jnp.float32
BF16 = jnp.bfloat16


def fit(values, degree):
    cheb = np.polynomial.Chebyshev.interpolate(values, degree, domain=[0.0, 0.25])
    return [float(c) for c in cheb.convert(kind=np.polynomial.Polynomial).coef]


COS = fit(lambda u: np.cos(2 * np.pi * np.sqrt(u)), 6)
SIN = fit(lambda u: 2 * np.pi * np.sinc(2 * np.sqrt(u)), 6)


def onehot(size, source_of):
    row = lax.broadcasted_iota(jnp.int32, (size, size), 0)
    col = lax.broadcasted_iota(jnp.int32, (size, size), 1)
    return (col == source_of(row)).astype(F32).astype(BF16)


def regroup_kernel(v_ref, out_ref):
    perm = onehot(256, lambda r: (r & 15) * 16 + (r >> 4))
    for f in range(0, v_ref.shape[1], 16):
        rows = jnp.concatenate(
            [v_ref[part, f : f + 16].reshape(256, TIME) for part in range(2)], 1
        )
        moved = jnp.dot(perm, rows, preferred_element_type=F32).astype(BF16)
        for part in range(2):
            out_ref[:, part, f : f + 16, :] = moved[:, part * TIME : (part + 1) * TIME].reshape(
                16, 16, TIME
            )


def regroup(v):
    _, feeds, chans, time = v.shape
    return pl.pallas_call(
        regroup_kernel,
        grid=(chans // 16,),
        in_specs=[pl.BlockSpec((2, feeds, 16, time), lambda i: (0, 0, i, 0))],
        out_specs=pl.BlockSpec((16, 2, feeds, time), lambda i: (i, 0, 0, 0)),
        out_shape=jax.ShapeDtypeStruct((chans, 2, feeds, time), BF16),
        name="regroup",
    )(v)


def weights_kernel(chan_ref, beam_ref, feed_ref, out_ref, turns_ref):
    factor = (chan_ref[0] + pl.program_id(0) + 400) % 4096
    bm = beam_ref.shape[1]

    def rows_of(ref):
        row = lax.broadcasted_iota(jnp.int32, (16, ref.shape[1]), 0)
        return row, jnp.where(row < 2, ref[0:1, :], ref[1:2, :])

    row, grid = rows_of(beam_ref)
    part = (grid * factor) & 4095
    left = jnp.where((row & 1) == 0, part & 4032, part & 63)
    left = jnp.where(row < 4, left, 0).astype(F32).astype(BF16)
    right = rows_of(feed_ref)[1].astype(F32).astype(BF16)
    turns_ref[...] = lax.dot_general(
        left, right, (((0,), (0,)), ((), ())), preferred_element_type=F32
    )
    scale = 1.0 / math.sqrt(FEEDS)
    width = 512

    def chunk(i, carry):
        r0 = pl.multiple_of(i * 16, 16)
        for c0 in range(0, FEEDS, width):
            t = turns_ref[pl.ds(r0, 16), c0 : c0 + width] * (1.0 / 4096.0)
            r = t - jnp.round(t)
            u = r * r
            c = COS[-1] * scale
            for coef in COS[-2::-1]:
                c = c * u + coef * scale
            s = -SIN[-1] * scale
            for coef in SIN[-2::-1]:
                s = s * u - coef * scale
            out_ref[0, pl.ds(r0, 16), c0 : c0 + width] = c.astype(BF16)
            out_ref[0, pl.ds(r0, 16), FEEDS + c0 : FEEDS + c0 + width] = (s * r).astype(BF16)
        return carry

    lax.fori_loop(0, bm // 16, chunk, 0)


def weights(first_chan, beam_grid, feed_pos, local_chans):
    bm = 128
    return pl.pallas_call(
        weights_kernel,
        grid=(local_chans, BEAMS // bm),
        in_specs=[
            pl.BlockSpec(memory_space=pltpu.SMEM),
            pl.BlockSpec((2, bm), lambda c, m: (0, m)),
            pl.BlockSpec((2, FEEDS), lambda c, m: (0, 0)),
        ],
        out_specs=pl.BlockSpec((1, bm, 2 * FEEDS), lambda c, m: (c, m, 0)),
        out_shape=jax.ShapeDtypeStruct((local_chans, BEAMS, 2 * FEEDS), BF16),
        scratch_shapes=[pltpu.VMEM((bm, FEEDS), F32)],
        compiler_params=pltpu.CompilerParams(vmem_limit_bytes=24 * 2**20),
        cost_estimate=pl.CostEstimate(
            flops=30 * local_chans * BEAMS * FEEDS * 20,
            bytes_accessed=local_chans * BEAMS * FEEDS * 4,
            transcendentals=0,
        ),
        name="weights",
    )(first_chan, beam_grid.T, feed_pos.T)


def split(x):
    high = x.astype(BF16)
    return high, (x - high.astype(F32)).astype(BF16)


def beams_kernel(w_ref, v_ref, table_ref, flags_ref, out_ref, rhs_ref, inten_ref, sum_ref, power_ref):
    chan, step = pl.program_id(0), pl.program_id(1)
    bm = w_ref.shape[1]

    @pl.when(step == 0)
    def _():
        real = v_ref[:, chan, 0].reshape(FEEDS, TIME)
        imag = v_ref[:, chan, 1].reshape(FEEDS, TIME)
        rhs_ref[:FEEDS, :TIME] = real
        rhs_ref[:FEEDS, TIME:] = imag
        rhs_ref[FEEDS:, :TIME] = -imag
        rhs_ref[FEEDS:, TIME:] = real
        sum_ref[...] = jnp.zeros_like(sum_ref)

    beam = jnp.dot(w_ref[0], rhs_ref[...], preferred_element_type=F32)
    high, low = split(beam)
    size = 2 * TIME
    fine = (
        jnp.dot(high, table_ref[:size], preferred_element_type=F32)
        + jnp.dot(high, table_ref[size:], preferred_element_type=F32)
        + jnp.dot(low, table_ref[:size], preferred_element_type=F32)
    )
    real, imag = fine[:, :TIME], fine[:, TIME:]
    intensity = real * real + imag * imag
    inten_ref[pl.ds(pl.multiple_of(step * bm, bm), bm), :] = intensity
    sum_ref[...] += jnp.sum(intensity.reshape(bm // 8, 8, TIME), axis=0)

    @pl.when(step == pl.num_programs(1) - 1)
    def _():
        total = jnp.broadcast_to(jnp.sum(sum_ref[...], axis=0, keepdims=True), (8, TIME))
        for shift in (64, 32, 16):
            total = total + pltpu.roll(total, shift, 1)
        bandpass = total[0:1] * (1.0 / (BEAMS * TOUT)) + 1e-06
        scale = flags_ref[pl.ds(chan, 1), :] / bandpass
        power_ref[chan] = (inten_ref[...] * scale).astype(BF16)

    @pl.when((step == pl.num_programs(1) - 1) & (chan == 1))
    def _():
        perm = onehot(256, lambda r: ((r >> 1) & 1) * 128 + (r >> 2) * 2 + (r & 1))
        for i in range(BEAMS // 128):
            pair = power_ref[:, i * 128 : (i + 1) * 128, :].reshape(256, TIME)
            out_ref[i * 256 : (i + 1) * 256, :] = jnp.dot(
                perm, pair, preferred_element_type=F32
            ).astype(BF16)


def dft_table():
    n = np.arange(TIME)
    same = n[:, None] // UPCHAN == n[None, :] // UPCHAN
    angle = 2 * np.pi * ((n[:, None] * n[None, :]) % UPCHAN) / UPCHAN
    cos, sin = np.cos(angle) * same / 4.0, np.sin(angle) * same / 4.0
    table = np.block([[cos, -sin], [sin, cos]]).astype(np.float32)
    high = table.astype(jnp.bfloat16)
    low = (table - high.astype(np.float32)).astype(jnp.bfloat16)
    return np.concatenate([high, low], 0)


def form_beams(w, v, flags):
    bm = 256
    return pl.pallas_call(
        beams_kernel,
        grid=(2, BEAMS // bm),
        in_specs=[
            pl.BlockSpec((1, bm, 2 * FEEDS), lambda c, m: (c, m, 0)),
            pl.BlockSpec(v.shape, lambda c, m: (0, 0, 0, 0, 0)),
            pl.BlockSpec((4 * TIME, 2 * TIME), lambda c, m: (0, 0)),
            pl.BlockSpec((2, TIME), lambda c, m: (0, 0)),
        ],
        out_specs=pl.BlockSpec((2 * BEAMS, TIME), lambda c, m: (0, 0)),
        out_shape=jax.ShapeDtypeStruct((2 * BEAMS, TIME), BF16),
        scratch_shapes=[
            pltpu.VMEM((2 * FEEDS, 2 * TIME), BF16),
            pltpu.VMEM((BEAMS, TIME), F32),
            pltpu.VMEM((8, TIME), F32),
            pltpu.VMEM((2, BEAMS, TIME), BF16),
        ],
        compiler_params=pltpu.CompilerParams(vmem_limit_bytes=32 * 2**20),
        name="beams",
    )(w, v, jnp.asarray(dft_table()), flags)


def finish_kernel(in_ref, power_ref, sums_ref):
    def gather_from(r):
        combo = (r >> 6) * 8 + (r & 7)
        eighth = (r >> 3) & 7
        return (eighth >> 1) * 64 + (combo >> 1) * 4 + (eighth & 1) * 2 + (combo & 1)

    def scatter_from(r):
        combo = r >> 3
        return (combo >> 3) * 64 + (r & 7) * 8 + (combo & 7)

    first, second = onehot(256, gather_from), onehot(256, scatter_from)
    lane = lax.broadcasted_iota(jnp.int32, (8, TIME), 1)
    for q in range(8):
        x = jnp.dot(first, in_ref[q * 256 : (q + 1) * 256, :], preferred_element_type=F32)
        blocks = []
        for group in range(4):
            tiles = [x[group * 64 + i * 8 : group * 64 + i * 8 + 8, :] for i in range(8)]
            for bit in (1, 2, 4):
                upper = (lane & (16 * bit)) != 0
                for i in range(8):
                    if i & bit == 0:
                        low, high = tiles[i], tiles[i | bit]
                        tiles[i] = jnp.where(upper, pltpu.roll(high, 16 * bit, 1), low)
                        tiles[i | bit] = jnp.where(upper, high, pltpu.roll(low, TIME - 16 * bit, 1))
            total = sum(tiles[1:], tiles[0])
            squares = sum([t * t for t in tiles[1:]], tiles[0] * tiles[0])
            for member in range(4):
                gy = group * 4 + member
                at = (gy * 8 + q) * TIME
                sums_ref[0, :, at : at + TIME] = total[2 * member : 2 * member + 2, :]
                sums_ref[1, :, at : at + TIME] = squares[2 * member : 2 * member + 2, :]
            blocks += tiles
        y = jnp.concatenate(blocks, 0).astype(BF16)
        z = jnp.dot(second, y, preferred_element_type=F32).astype(BF16)
        for gy in range(16):
            at = (gy * 8 + q) * TIME
            for beam in range(2):
                row = gy * 16 + beam * 8
                power_ref[beam, :, at : at + TIME] = z[row : row + 8, :]


def finish(received):
    freqs = 512 * 2 * UPCHAN
    return pl.pallas_call(
        finish_kernel,
        out_shape=(
            jax.ShapeDtypeStruct((2, TOUT, freqs), BF16),
            jax.ShapeDtypeStruct((2, 2, freqs), F32),
        ),
        compiler_params=pltpu.CompilerParams(vmem_limit_bytes=24 * 2**20),
        name="finish",
    )(received)


def per_device(voltages, beam_grid, feed_pos, rfi_mask):
    inputs = lax.axis_size("gx")
    chan_dev = voltages.shape[2]
    local_chans = chan_dev // inputs
    first_chan = lax.axis_index("gy") * chan_dev + lax.axis_index("gx") * local_chans
    sent = regroup(voltages)
    piece = lax.all_to_all(sent, "gx", split_axis=0, concat_axis=0, tiled=True)
    w = weights(first_chan.reshape(1).astype(jnp.int32), beam_grid, feed_pos, local_chans)
    flags = rfi_mask.reshape(TOUT, local_chans, UPCHAN).transpose(1, 0, 2).astype(F32)
    piece = piece.reshape(inputs, local_chans, 2, voltages.shape[1], TIME)
    power = form_beams(w, piece, flags.reshape(local_chans, TIME))
    power = power.reshape(512, 4, TIME)
    power = lax.all_to_all(power, ("gx", "gy"), split_axis=0, concat_axis=0, tiled=True)
    return finish(power.reshape(2048, TIME))


def solution(mesh):
    in_specs = (P(None, "gx", "gy", None), P(), P(), P(None, ("gy", "gx")))
    out_specs = (P(("gx", "gy"), None, None), P(None, ("gx", "gy"), None))
    return jax.shard_map(
        per_device, mesh=mesh, in_specs=in_specs, out_specs=out_specs, check_vma=False
    )
```

```python
import math

import jax
import jax.numpy as jnp
import numpy as np
from jax import lax
from jax.experimental import pallas as pl
from jax.experimental.pallas import tpu as pltpu
from jax.sharding import PartitionSpec as P

FEEDS = 2048
BEAMS = 1024
UPCHAN = 16
TOUT = 8
TIME = 128
F32 = jnp.float32
BF16 = jnp.bfloat16


def fit(values, degree):
    cheb = np.polynomial.Chebyshev.interpolate(values, degree, domain=[0.0, 0.25])
    return [float(c) for c in cheb.convert(kind=np.polynomial.Polynomial).coef]


COS = fit(lambda u: np.cos(2 * np.pi * np.sqrt(u)), 6)
SIN = fit(lambda u: 2 * np.pi * np.sinc(2 * np.sqrt(u)), 6)


def onehot(size, source_of):
    row = lax.broadcasted_iota(jnp.int32, (size, size), 0)
    col = lax.broadcasted_iota(jnp.int32, (size, size), 1)
    return (col == source_of(row)).astype(F32).astype(BF16)


def regroup_kernel(v_ref, out_ref, in_buf, out_buf, in_sem, out_sem):
    parts, feeds, chans, _ = v_ref.shape
    pieces = [(part, f) for f in range(0, feeds, 16) for part in range(parts)]

    def fetch(n):
        at = (pieces[n][0], pl.ds(pieces[n][1], 16))
        return pltpu.make_async_copy(v_ref.at[at], in_buf.at[at], in_sem.at[n])

    def store(n):
        at = (slice(None), pieces[n][0], pl.ds(pieces[n][1], 16))
        return pltpu.make_async_copy(out_buf.at[at], out_ref.at[at], out_sem.at[n])

    for n in range(len(pieces)):
        fetch(n).start()
    for n, (part, f) in enumerate(pieces):
        fetch(n).wait()
        for c in range(0, chans, 16):
            tile = in_buf[part, f : f + 16, c : c + 16]
            out_buf[c : c + 16, part, f : f + 16, :] = jnp.swapaxes(tile, 0, 1)
        store(n).start()
    for n in range(len(pieces)):
        store(n).wait()


def regroup(v):
    parts, feeds, chans, time = v.shape
    count = parts * feeds // 16
    return pl.pallas_call(
        regroup_kernel,
        in_specs=[pl.BlockSpec(memory_space=pltpu.HBM)],
        out_specs=pl.BlockSpec(memory_space=pltpu.HBM),
        out_shape=jax.ShapeDtypeStruct((chans, parts, feeds, time), BF16),
        scratch_shapes=[
            pltpu.VMEM(v.shape, BF16),
            pltpu.VMEM((chans, parts, feeds, time), BF16),
            pltpu.SemaphoreType.DMA((count,)),
            pltpu.SemaphoreType.DMA((count,)),
        ],
        compiler_params=pltpu.CompilerParams(vmem_limit_bytes=16 * 2**20),
        name="regroup",
    )(pltpu.with_memory_space_constraint(v, pltpu.HBM))


def weights_kernel(chan_ref, beam_ref, feed_ref, out_ref, turns_ref):
    factor = (chan_ref[0] + pl.program_id(0) + 400) % 4096
    bm = beam_ref.shape[1]

    def rows_of(ref):
        row = lax.broadcasted_iota(jnp.int32, (16, ref.shape[1]), 0)
        return row, jnp.where(row < 2, ref[0:1, :], ref[1:2, :])

    row, grid = rows_of(beam_ref)
    part = (grid * factor) & 4095
    left = jnp.where((row & 1) == 0, part & 4032, part & 63)
    left = jnp.where(row < 4, left, 0).astype(F32).astype(BF16)
    right = rows_of(feed_ref)[1].astype(F32).astype(BF16)
    turns_ref[...] = lax.dot_general(
        left, right, (((0,), (0,)), ((), ())), preferred_element_type=F32
    )
    scale = 1.0 / math.sqrt(FEEDS)
    width = 512

    def chunk(i, carry):
        r0 = pl.multiple_of(i * 16, 16)
        for c0 in range(0, FEEDS, width):
            t = turns_ref[pl.ds(r0, 16), c0 : c0 + width] * (1.0 / 4096.0)
            r = t - jnp.round(t)
            u = r * r
            c = COS[-1] * scale
            for coef in COS[-2::-1]:
                c = c * u + coef * scale
            s = -SIN[-1] * scale
            for coef in SIN[-2::-1]:
                s = s * u - coef * scale
            out_ref[0, pl.ds(r0, 16), c0 : c0 + width] = c.astype(BF16)
            out_ref[0, pl.ds(r0, 16), FEEDS + c0 : FEEDS + c0 + width] = (s * r).astype(BF16)
        return carry

    lax.fori_loop(0, bm // 16, chunk, 0)


def weights(first_chan, beam_grid, feed_pos, local_chans):
    bm = 128
    return pl.pallas_call(
        weights_kernel,
        grid=(local_chans, BEAMS // bm),
        in_specs=[
            pl.BlockSpec(memory_space=pltpu.SMEM),
            pl.BlockSpec((2, bm), lambda c, m: (0, m)),
            pl.BlockSpec((2, FEEDS), lambda c, m: (0, 0)),
        ],
        out_specs=pl.BlockSpec((1, bm, 2 * FEEDS), lambda c, m: (c, m, 0)),
        out_shape=pltpu.HBM((local_chans, BEAMS, 2 * FEEDS), BF16),
        scratch_shapes=[pltpu.VMEM((bm, FEEDS), F32)],
        compiler_params=pltpu.CompilerParams(vmem_limit_bytes=24 * 2**20),
        cost_estimate=pl.CostEstimate(
            flops=30 * local_chans * BEAMS * FEEDS * 20,
            bytes_accessed=local_chans * BEAMS * FEEDS * 4,
            transcendentals=0,
        ),
        name="weights",
    )(first_chan, beam_grid.T, feed_pos.T)


def split(x):
    high = x.astype(BF16)
    return high, (x - high.astype(F32)).astype(BF16)


def beams_kernel(
    w_hbm, v_ref, table_ref, flags_ref, out_ref, w_buf, sem, rhs_ref, beam_ref, inten_ref, rows_ref
):
    slots, bm, _ = w_buf.shape
    steps = BEAMS // bm
    size = 2 * TIME

    def fetch(i):
        rows = pl.ds(pl.multiple_of(i % steps * bm, bm), bm)
        return pltpu.make_async_copy(w_hbm.at[i // steps, rows], w_buf.at[i % slots], sem.at[i % slots])

    for i in range(slots):
        fetch(i).start()
    for chan in range(2):
        real = v_ref[:, chan, 0].reshape(FEEDS, TIME)
        imag = v_ref[:, chan, 1].reshape(FEEDS, TIME)
        rhs_ref[chan, :FEEDS, :TIME] = real
        rhs_ref[chan, :FEEDS, TIME:] = imag
        rhs_ref[chan, FEEDS:, :TIME] = -imag
        rhs_ref[chan, FEEDS:, TIME:] = real
    beam_ref[1] = jnp.zeros_like(beam_ref[1])

    def detect(i):
        high, low = split(beam_ref[i % 2])
        fine = (
            jnp.dot(high, table_ref[:size], preferred_element_type=F32)
            + jnp.dot(high, table_ref[size:], preferred_element_type=F32)
            + jnp.dot(low, table_ref[:size], preferred_element_type=F32)
        )
        real, imag = fine[:, :TIME], fine[:, TIME:]
        rows = pl.ds(pl.multiple_of(i % steps * bm, bm), bm)
        inten_ref[i // steps, rows, :] = real * real + imag * imag

    def normalize(chan):
        def add(j, total):
            x = inten_ref[chan, pl.ds(pl.multiple_of(j * 128, 128), 128), :]
            return total + jnp.sum(x.reshape(16, 8, TIME), axis=0)

        total = lax.fori_loop(0, BEAMS // 128, add, jnp.zeros((8, TIME), F32))
        total = jnp.broadcast_to(jnp.sum(total, axis=0, keepdims=True), (8, TIME))
        for shift in (64, 32, 16):
            total = total + pltpu.roll(total, shift, 1)
        bandpass = total[0:1] * (1.0 / (BEAMS * TOUT)) + 1e-06
        scale = flags_ref[chan : chan + 1, :] / bandpass

        def move(j, carry):
            for beam in range(2):
                x = inten_ref[chan, pl.ds(j * 128 + beam, 64, stride=2), :]
                rows_ref[pl.ds(j * 256 + 2 * chan + beam, 64, stride=4), :] = x * scale
            if chan == 1:
                rows = pl.ds(pl.multiple_of(j * 256, 256), 256)
                out_ref[rows, :] = rows_ref[rows, :].astype(BF16)
            return carry

        lax.fori_loop(0, BEAMS // 128, move, 0)

    def body(i, carry):
        fetch(i).wait()
        beam = jnp.dot(w_buf[i % slots], rhs_ref[i // steps], preferred_element_type=F32)
        detect(jnp.maximum(i - 1, 0))
        beam_ref[i % 2] = beam

        @pl.when(i + slots < 2 * steps)
        def _():
            fetch(i + slots).start()

        @pl.when(i == steps)
        def _():
            normalize(0)

        return carry

    lax.fori_loop(0, 2 * steps, body, 0)
    detect(2 * steps - 1)
    normalize(1)


def dft_table():
    n = np.arange(TIME)
    same = n[:, None] // UPCHAN == n[None, :] // UPCHAN
    angle = 2 * np.pi * ((n[:, None] * n[None, :]) % UPCHAN) / UPCHAN
    cos, sin = np.cos(angle) * same / 4.0, np.sin(angle) * same / 4.0
    table = np.block([[cos, -sin], [sin, cos]]).astype(np.float32)
    high = table.astype(jnp.bfloat16)
    low = (table - high.astype(np.float32)).astype(jnp.bfloat16)
    return np.concatenate([high, low], 0)


def form_beams(w, v, flags):
    bm, slots = 256, 4
    vmem = pl.BlockSpec(memory_space=pltpu.VMEM)
    return pl.pallas_call(
        beams_kernel,
        in_specs=[pl.BlockSpec(memory_space=pltpu.HBM), vmem, vmem, vmem],
        out_specs=vmem,
        out_shape=jax.ShapeDtypeStruct((2 * BEAMS, TIME), BF16),
        scratch_shapes=[
            pltpu.VMEM((slots, bm, 2 * FEEDS), BF16),
            pltpu.SemaphoreType.DMA((slots,)),
            pltpu.VMEM((2, 2 * FEEDS, 2 * TIME), BF16),
            pltpu.VMEM((2, bm, 2 * TIME), F32),
            pltpu.VMEM((2, BEAMS, TIME), F32),
            pltpu.VMEM((2 * BEAMS, TIME), F32),
        ],
        compiler_params=pltpu.CompilerParams(vmem_limit_bytes=32 * 2**20),
        name="beams",
    )(pltpu.with_memory_space_constraint(w, pltpu.HBM), v, jnp.asarray(dft_table()), flags)


def finish_kernel(in_ref, power_ref, sums_ref):
    def gather_from(r):
        combo = (r >> 6) * 8 + (r & 7)
        eighth = (r >> 3) & 7
        return (eighth >> 1) * 64 + (combo >> 1) * 4 + (eighth & 1) * 2 + (combo & 1)

    def scatter_from(r):
        combo = r >> 3
        return (combo >> 3) * 64 + (r & 7) * 8 + (combo & 7)

    first, second = onehot(256, gather_from), onehot(256, scatter_from)
    lane = lax.broadcasted_iota(jnp.int32, (8, TIME), 1)
    for q in range(8):
        x = jnp.dot(first, in_ref[q * 256 : (q + 1) * 256, :], preferred_element_type=F32)
        blocks = []
        for group in range(4):
            tiles = [x[group * 64 + i * 8 : group * 64 + i * 8 + 8, :] for i in range(8)]
            for bit in (1, 2, 4):
                upper = (lane & (16 * bit)) != 0
                for i in range(8):
                    if i & bit == 0:
                        low, high = tiles[i], tiles[i | bit]
                        tiles[i] = jnp.where(upper, pltpu.roll(high, 16 * bit, 1), low)
                        tiles[i | bit] = jnp.where(upper, high, pltpu.roll(low, TIME - 16 * bit, 1))
            total = sum(tiles[1:], tiles[0])
            squares = sum([t * t for t in tiles[1:]], tiles[0] * tiles[0])
            for member in range(4):
                gy = group * 4 + member
                at = (gy * 8 + q) * TIME
                sums_ref[0, :, at : at + TIME] = total[2 * member : 2 * member + 2, :]
                sums_ref[1, :, at : at + TIME] = squares[2 * member : 2 * member + 2, :]
            blocks += tiles
        y = jnp.concatenate(blocks, 0).astype(BF16)
        z = jnp.dot(second, y, preferred_element_type=F32).astype(BF16)
        for gy in range(16):
            at = (gy * 8 + q) * TIME
            for beam in range(2):
                row = gy * 16 + beam * 8
                power_ref[beam, :, at : at + TIME] = z[row : row + 8, :]


def finish(received):
    freqs = 512 * 2 * UPCHAN
    return pl.pallas_call(
        finish_kernel,
        out_shape=(
            jax.ShapeDtypeStruct((2, TOUT, freqs), BF16),
            jax.ShapeDtypeStruct((2, 2, freqs), F32),
        ),
        compiler_params=pltpu.CompilerParams(vmem_limit_bytes=24 * 2**20),
        name="finish",
    )(received)


def per_device(voltages, beam_grid, feed_pos, rfi_mask):
    inputs = lax.axis_size("gx")
    chan_dev = voltages.shape[2]
    local_chans = chan_dev // inputs
    first_chan = lax.axis_index("gy") * chan_dev + lax.axis_index("gx") * local_chans
    sent = regroup(voltages)
    piece = lax.all_to_all(sent, "gx", split_axis=0, concat_axis=0, tiled=True)
    w = weights(first_chan.reshape(1).astype(jnp.int32), beam_grid, feed_pos, local_chans)
    flags = rfi_mask.reshape(TOUT, local_chans, UPCHAN).transpose(1, 0, 2).astype(F32)
    piece = piece.reshape(inputs, local_chans, 2, voltages.shape[1], TIME)
    power = form_beams(w, piece, flags.reshape(local_chans, TIME))
    power = power.reshape(512, 4, TIME)
    power = lax.all_to_all(power, ("gx", "gy"), split_axis=0, concat_axis=0, tiled=True)
    return finish(power.reshape(2048, TIME))


def solution(mesh):
    in_specs = (P(None, "gx", "gy", None), P(), P(), P(None, ("gy", "gx")))
    out_specs = (P(("gx", "gy"), None, None), P(None, ("gx", "gy"), None))
    return jax.shard_map(
        per_device, mesh=mesh, in_specs=in_specs, out_specs=out_specs, check_vma=False
    )
```

```python
import functools
import math

import jax
import jax.numpy as jnp
import numpy as np
from jax import lax
from jax.experimental import pallas as pl
from jax.experimental.pallas import tpu as pltpu
from jax.sharding import PartitionSpec as P

FEEDS = 2048
BEAMS = 1024
UPCHAN = 16
TOUT = 8
TIME = 128
F32 = jnp.float32
BF16 = jnp.bfloat16


def fit(values, degree):
    cheb = np.polynomial.Chebyshev.interpolate(values, degree, domain=[0.0, 0.25])
    return [float(c) for c in cheb.convert(kind=np.polynomial.Polynomial).coef]


COS = fit(lambda u: np.cos(2 * np.pi * np.sqrt(u)), 6)
SIN = fit(lambda u: 2 * np.pi * np.sinc(2 * np.sqrt(u)), 6)


def onehot(size, source_of):
    row = lax.broadcasted_iota(jnp.int32, (size, size), 0)
    col = lax.broadcasted_iota(jnp.int32, (size, size), 1)
    return (col == source_of(row)).astype(F32).astype(BF16)


def regroup_kernel(v_ref, out_ref, in_buf, out_buf, in_sem, out_sem):
    parts, feeds, chans, _ = v_ref.shape
    pieces = [(part, f) for f in range(0, feeds, 16) for part in range(parts)]

    def fetch(n):
        at = (pieces[n][0], pl.ds(pieces[n][1], 16))
        return pltpu.make_async_copy(v_ref.at[at], in_buf.at[at], in_sem.at[n])

    def store(n):
        at = (slice(None), pieces[n][0], pl.ds(pieces[n][1], 16))
        return pltpu.make_async_copy(out_buf.at[at], out_ref.at[at], out_sem.at[n])

    for n in range(len(pieces)):
        fetch(n).start()
    for n, (part, f) in enumerate(pieces):
        fetch(n).wait()
        for c in range(0, chans, 16):
            tile = in_buf[part, f : f + 16, c : c + 16]
            out_buf[c : c + 16, part, f : f + 16, :] = jnp.swapaxes(tile, 0, 1)
        store(n).start()
    for n in range(len(pieces)):
        store(n).wait()


def regroup(v):
    parts, feeds, chans, time = v.shape
    count = parts * feeds // 16
    return pl.pallas_call(
        regroup_kernel,
        in_specs=[pl.BlockSpec(memory_space=pltpu.HBM)],
        out_specs=pl.BlockSpec(memory_space=pltpu.HBM),
        out_shape=pltpu.HBM((chans, parts, feeds, time), BF16),
        scratch_shapes=[
            pltpu.VMEM(v.shape, BF16),
            pltpu.VMEM((chans, parts, feeds, time), BF16),
            pltpu.SemaphoreType.DMA((count,)),
            pltpu.SemaphoreType.DMA((count,)),
        ],
        compiler_params=pltpu.CompilerParams(vmem_limit_bytes=16 * 2**20),
        name="regroup",
    )(pltpu.with_memory_space_constraint(v, pltpu.HBM))


def weights_kernel(local_chans, beam_ref, feed_ref, out_ref, turns_ref):
    device = lax.axis_index("gy") * lax.axis_size("gx") + lax.axis_index("gx")
    factor = (device * local_chans + pl.program_id(0) + 400) % 4096
    bm = beam_ref.shape[1]

    def rows_of(ref):
        row = lax.broadcasted_iota(jnp.int32, (16, ref.shape[1]), 0)
        return row, jnp.where(row < 2, ref[0:1, :], ref[1:2, :])

    row, grid = rows_of(beam_ref)
    part = (grid * factor) & 4095
    left = jnp.where((row & 1) == 0, part & 4032, part & 63)
    left = jnp.where(row < 4, left, 0).astype(F32).astype(BF16)
    right = rows_of(feed_ref)[1].astype(F32).astype(BF16)
    turns_ref[...] = lax.dot_general(
        left, right, (((0,), (0,)), ((), ())), preferred_element_type=F32
    )
    scale = 1.0 / math.sqrt(FEEDS)
    width = 512

    def chunk(i, carry):
        r0 = pl.multiple_of(i * 16, 16)
        for c0 in range(0, FEEDS, width):
            t = turns_ref[pl.ds(r0, 16), c0 : c0 + width] * (1.0 / 4096.0)
            r = t - jnp.round(t)
            u = r * r
            c = COS[-1] * scale
            for coef in COS[-2::-1]:
                c = c * u + coef * scale
            s = -SIN[-1] * scale
            for coef in SIN[-2::-1]:
                s = s * u - coef * scale
            out_ref[0, pl.ds(r0, 16), c0 : c0 + width] = c.astype(BF16)
            out_ref[0, pl.ds(r0, 16), FEEDS + c0 : FEEDS + c0 + width] = (s * r).astype(BF16)
        return carry

    lax.fori_loop(0, bm // 16, chunk, 0)


def weights(beam_grid, feed_pos, local_chans):
    bm = 128
    return pl.pallas_call(
        functools.partial(weights_kernel, local_chans),
        grid=(local_chans, BEAMS // bm),
        in_specs=[
            pl.BlockSpec((2, bm), lambda c, m: (0, m)),
            pl.BlockSpec((2, FEEDS), lambda c, m: (0, 0)),
        ],
        out_specs=pl.BlockSpec((1, bm, 2 * FEEDS), lambda c, m: (c, m, 0)),
        out_shape=pltpu.HBM((local_chans, BEAMS, 2 * FEEDS), BF16),
        scratch_shapes=[pltpu.VMEM((bm, FEEDS), F32)],
        compiler_params=pltpu.CompilerParams(vmem_limit_bytes=24 * 2**20),
        cost_estimate=pl.CostEstimate(
            flops=30 * local_chans * BEAMS * FEEDS * 20,
            bytes_accessed=local_chans * BEAMS * FEEDS * 4,
            transcendentals=0,
        ),
        name="weights",
    )(beam_grid.T, feed_pos.T)


def split(x):
    high = x.astype(BF16)
    return high, (x - high.astype(F32)).astype(BF16)


def beams_kernel(
    w_hbm, v_ref, table_ref, flags_ref, out_ref, w_buf, sem, rhs_ref, beam_ref, inten_ref, rows_ref, sum_ref
):
    slots, bm, _ = w_buf.shape
    steps = BEAMS // bm
    size = 2 * TIME

    def fetch(i):
        rows = pl.ds(pl.multiple_of(i % steps * bm, bm), bm)
        return pltpu.make_async_copy(w_hbm.at[i // steps, rows], w_buf.at[i % slots], sem.at[i % slots])

    for i in range(slots):
        fetch(i).start()
    for chan in range(2):
        real = v_ref[:, chan, 0].reshape(FEEDS, TIME)
        imag = v_ref[:, chan, 1].reshape(FEEDS, TIME)
        rhs_ref[chan, :FEEDS, :TIME] = real
        rhs_ref[chan, :FEEDS, TIME:] = imag
        rhs_ref[chan, FEEDS:, :TIME] = -imag
        rhs_ref[chan, FEEDS:, TIME:] = real
    beam_ref[1] = jnp.zeros_like(beam_ref[1])

    def detect(i):
        high, low = split(beam_ref[i % 2])
        fine = (
            jnp.dot(high, table_ref[:size], preferred_element_type=F32)
            + jnp.dot(high, table_ref[size:], preferred_element_type=F32)
            + jnp.dot(low, table_ref[:size], preferred_element_type=F32)
        )
        real, imag = fine[:, :TIME], fine[:, TIME:]
        rows = pl.ds(pl.multiple_of(i % steps * bm, bm), bm)
        x = real * real + imag * imag
        inten_ref[i // steps, rows, :] = x
        sum_ref[i] = jnp.sum(x.reshape(bm // 8, 8, TIME), axis=0)

    def normalize(chan):
        total = jnp.sum(sum_ref[chan * steps : (chan + 1) * steps], axis=0)
        total = jnp.broadcast_to(jnp.sum(total, axis=0, keepdims=True), (8, TIME))
        for shift in (64, 32, 16):
            total = total + pltpu.roll(total, shift, 1)
        bandpass = total[0:1] * (1.0 / (BEAMS * TOUT)) + 1e-06
        scale = flags_ref[chan : chan + 1, :] / bandpass

        def move(j, carry):
            for beam in range(2):
                x = inten_ref[chan, pl.ds(j * 128 + beam, 64, stride=2), :]
                rows_ref[pl.ds(j * 256 + 2 * chan + beam, 64, stride=4), :] = x * scale
            if chan == 1:
                rows = pl.ds(pl.multiple_of(j * 256, 256), 256)
                out_ref[rows, :] = rows_ref[rows, :].astype(BF16)
            return carry

        lax.fori_loop(0, BEAMS // 128, move, 0, unroll=True)

    def body(i, carry):
        fetch(i).wait()
        beam = jnp.dot(w_buf[i % slots], rhs_ref[i // steps], preferred_element_type=F32)
        detect(jnp.maximum(i - 1, 0))
        beam_ref[i % 2] = beam

        @pl.when(i + slots < 2 * steps)
        def _():
            fetch(i + slots).start()

        @pl.when(i == steps)
        def _():
            normalize(0)

        return carry

    lax.fori_loop(0, 2 * steps, body, 0)
    detect(2 * steps - 1)
    normalize(1)


def dft_table():
    n = np.arange(TIME)
    same = n[:, None] // UPCHAN == n[None, :] // UPCHAN
    angle = 2 * np.pi * ((n[:, None] * n[None, :]) % UPCHAN) / UPCHAN
    cos, sin = np.cos(angle) * same / 4.0, np.sin(angle) * same / 4.0
    table = np.block([[cos, -sin], [sin, cos]]).astype(np.float32)
    high = table.astype(jnp.bfloat16)
    low = (table - high.astype(np.float32)).astype(jnp.bfloat16)
    return np.concatenate([high, low], 0)


def form_beams(w, v, flags):
    bm, slots = 256, 4
    vmem = pl.BlockSpec(memory_space=pltpu.VMEM)
    return pl.pallas_call(
        beams_kernel,
        in_specs=[pl.BlockSpec(memory_space=pltpu.HBM), vmem, vmem, vmem],
        out_specs=vmem,
        out_shape=jax.ShapeDtypeStruct((2 * BEAMS, TIME), BF16),
        scratch_shapes=[
            pltpu.VMEM((slots, bm, 2 * FEEDS), BF16),
            pltpu.SemaphoreType.DMA((slots,)),
            pltpu.VMEM((2, 2 * FEEDS, 2 * TIME), BF16),
            pltpu.VMEM((2, bm, 2 * TIME), F32),
            pltpu.VMEM((2, BEAMS, TIME), F32),
            pltpu.VMEM((2 * BEAMS, TIME), F32),
            pltpu.VMEM((2 * BEAMS // bm, 8, TIME), F32),
        ],
        compiler_params=pltpu.CompilerParams(vmem_limit_bytes=32 * 2**20),
        name="beams",
    )(pltpu.with_memory_space_constraint(w, pltpu.HBM), v, jnp.asarray(dft_table()), flags)


def finish_kernel(in_ref, power_ref, sums_ref):
    def gather_from(r):
        combo = (r >> 6) * 8 + (r & 7)
        eighth = (r >> 3) & 7
        return (eighth >> 1) * 64 + (combo >> 1) * 4 + (eighth & 1) * 2 + (combo & 1)

    def scatter_from(r):
        combo = r >> 3
        return (combo >> 3) * 64 + (r & 7) * 8 + (combo & 7)

    first, second = onehot(256, gather_from), onehot(256, scatter_from)
    lane = lax.broadcasted_iota(jnp.int32, (8, TIME), 1)
    for q in range(8):
        x = jnp.dot(first, in_ref[q * 256 : (q + 1) * 256, :], preferred_element_type=F32)
        blocks = []
        for group in range(4):
            tiles = [x[group * 64 + i * 8 : group * 64 + i * 8 + 8, :] for i in range(8)]
            for bit in (1, 2, 4):
                upper = (lane & (16 * bit)) != 0
                for i in range(8):
                    if i & bit == 0:
                        low, high = tiles[i], tiles[i | bit]
                        tiles[i] = jnp.where(upper, pltpu.roll(high, 16 * bit, 1), low)
                        tiles[i | bit] = jnp.where(upper, high, pltpu.roll(low, TIME - 16 * bit, 1))
            total = sum(tiles[1:], tiles[0])
            squares = sum([t * t for t in tiles[1:]], tiles[0] * tiles[0])
            for member in range(4):
                gy = group * 4 + member
                at = (gy * 8 + q) * TIME
                sums_ref[0, :, at : at + TIME] = total[2 * member : 2 * member + 2, :]
                sums_ref[1, :, at : at + TIME] = squares[2 * member : 2 * member + 2, :]
            blocks += tiles
        y = jnp.concatenate(blocks, 0).astype(BF16)
        z = jnp.dot(second, y, preferred_element_type=F32).astype(BF16)
        for gy in range(16):
            at = (gy * 8 + q) * TIME
            for beam in range(2):
                row = gy * 16 + beam * 8
                power_ref[beam, :, at : at + TIME] = z[row : row + 8, :]


def finish(received):
    freqs = 512 * 2 * UPCHAN
    return pl.pallas_call(
        finish_kernel,
        out_shape=(
            jax.ShapeDtypeStruct((2, TOUT, freqs), BF16),
            jax.ShapeDtypeStruct((2, 2, freqs), F32),
        ),
        compiler_params=pltpu.CompilerParams(vmem_limit_bytes=24 * 2**20),
        name="finish",
    )(received)


def per_device(voltages, beam_grid, feed_pos, rfi_mask):
    inputs = lax.axis_size("gx")
    chan_dev = voltages.shape[2]
    local_chans = chan_dev // inputs
    sent = regroup(voltages)
    piece = lax.all_to_all(sent, "gx", split_axis=0, concat_axis=0, tiled=True)
    w = weights(beam_grid, feed_pos, local_chans)
    flags = rfi_mask.reshape(TOUT, local_chans, UPCHAN).transpose(1, 0, 2).astype(F32)
    piece = piece.reshape(inputs, local_chans, 2, voltages.shape[1], TIME)
    power = form_beams(w, piece, flags.reshape(local_chans, TIME))
    power = power.reshape(512, 4, TIME)
    power = lax.all_to_all(power, ("gx", "gy"), split_axis=0, concat_axis=0, tiled=True)
    return finish(power.reshape(2048, TIME))


def solution(mesh):
    in_specs = (P(None, "gx", "gy", None), P(), P(), P(None, ("gy", "gx")))
    out_specs = (P(("gx", "gy"), None, None), P(None, ("gx", "gy"), None))
    return jax.shard_map(
        per_device, mesh=mesh, in_specs=in_specs, out_specs=out_specs, check_vma=False
    )
```

```python
import functools
import math

import jax
import jax.numpy as jnp
import numpy as np
from jax import lax
from jax.experimental import pallas as pl
from jax.experimental.pallas import tpu as pltpu
from jax.sharding import PartitionSpec as P

FEEDS = 2048
BEAMS = 1024
UPCHAN = 16
TOUT = 8
TIME = 128
ROWS = 256
F32 = jnp.float32
BF16 = jnp.bfloat16


def fit(values, degree):
    cheb = np.polynomial.Chebyshev.interpolate(values, degree, domain=[0.0, 0.25])
    return [float(c) for c in cheb.convert(kind=np.polynomial.Polynomial).coef]


COS = fit(lambda u: np.cos(2 * np.pi * np.sqrt(u)), 6)
SIN = fit(lambda u: 2 * np.pi * np.sinc(2 * np.sqrt(u)), 6)


def onehot(size, source_of):
    row = lax.broadcasted_iota(jnp.int32, (size, size), 0)
    col = lax.broadcasted_iota(jnp.int32, (size, size), 1)
    return (col == source_of(row)).astype(F32).astype(BF16)


def regroup_kernel(v_ref, out_ref, in_buf, out_buf, in_sem, out_sem):
    parts, feeds, chans, time = v_ref.shape
    pieces = [(part, f) for f in range(0, feeds, 16) for part in range(parts)]

    def fetch(n):
        at = (pieces[n][0], pl.ds(pieces[n][1], 16))
        return pltpu.make_async_copy(v_ref.at[at], in_buf.at[at], in_sem.at[n])

    def store(n):
        at = (slice(None), pl.ds(n * 16, 16))
        return pltpu.make_async_copy(out_buf.at[at], out_ref.at[at], out_sem.at[n])

    for n in range(len(pieces)):
        fetch(n).start()
    for n, (part, f) in enumerate(pieces):
        fetch(n).wait()
        for c in range(0, chans, 16):
            tile = jnp.swapaxes(in_buf[part, f : f + 16, c : c + 16], 0, 1)
            out_buf[c : c + 16, f : f + 16, part * time : (part + 1) * time] = tile
        if part == parts - 1:
            store(f // 16).start()
    for n in range(feeds // 16):
        store(n).wait()


def regroup(v):
    parts, feeds, chans, time = v.shape
    shape = (chans, feeds, parts * time)
    return pl.pallas_call(
        regroup_kernel,
        in_specs=[pl.BlockSpec(memory_space=pltpu.HBM)],
        out_specs=pl.BlockSpec(memory_space=pltpu.HBM),
        out_shape=pltpu.HBM(shape, BF16),
        scratch_shapes=[
            pltpu.VMEM(v.shape, BF16),
            pltpu.VMEM(shape, BF16),
            pltpu.SemaphoreType.DMA((parts * feeds // 16,)),
            pltpu.SemaphoreType.DMA((feeds // 16,)),
        ],
        compiler_params=pltpu.CompilerParams(vmem_limit_bytes=16 * 2**20),
        name="regroup",
    )(pltpu.with_memory_space_constraint(v, pltpu.HBM))


def weights_kernel(local_chans, beam_ref, feed_ref, out_ref, turns_ref):
    device = lax.axis_index("gy") * lax.axis_size("gx") + lax.axis_index("gx")
    factor = (device * local_chans + pl.program_id(0) + 400) % 4096
    bm = beam_ref.shape[1]

    def rows_of(ref):
        row = lax.broadcasted_iota(jnp.int32, (16, ref.shape[1]), 0)
        return row, jnp.where(row < 2, ref[0:1, :], ref[1:2, :])

    row, grid = rows_of(beam_ref)
    part = (grid * factor) & 4095
    left = jnp.where((row & 1) == 0, part & 4032, part & 63)
    left = jnp.where(row < 4, left, 0).astype(F32).astype(BF16)
    right = rows_of(feed_ref)[1].astype(F32).astype(BF16)
    turns_ref[...] = lax.dot_general(
        left, right, (((0,), (0,)), ((), ())), preferred_element_type=F32
    )
    scale = 1.0 / math.sqrt(FEEDS)
    width = 512

    def chunk(i, carry):
        r0 = pl.multiple_of(i * 16, 16)
        for c0 in range(0, FEEDS, width):
            t = turns_ref[pl.ds(r0, 16), c0 : c0 + width] * (1.0 / 4096.0)
            r = t - jnp.round(t)
            u = r * r
            c = COS[-1] * scale
            for coef in COS[-2::-1]:
                c = c * u + coef * scale
            s = -SIN[-1] * scale
            for coef in SIN[-2::-1]:
                s = s * u - coef * scale
            out_ref[0, 0, 0, pl.ds(r0, 16), c0 : c0 + width] = c.astype(BF16)
            out_ref[0, 0, 1, pl.ds(r0, 16), c0 : c0 + width] = (s * r).astype(BF16)
        return carry

    lax.fori_loop(0, bm // 16, chunk, 0)


def weights(beam_grid, feed_pos, local_chans):
    bm = 128
    per = ROWS // bm
    return pl.pallas_call(
        functools.partial(weights_kernel, local_chans),
        grid=(local_chans, BEAMS // bm),
        in_specs=[
            pl.BlockSpec((2, bm), lambda c, m: (0, m)),
            pl.BlockSpec((2, FEEDS), lambda c, m: (0, 0)),
        ],
        out_specs=pl.BlockSpec((1, 1, 2, bm, FEEDS), lambda c, m: (c, m // per, 0, m % per, 0)),
        out_shape=pltpu.HBM((local_chans, BEAMS // ROWS, 2, ROWS, FEEDS), BF16),
        scratch_shapes=[pltpu.VMEM((bm, FEEDS), F32)],
        compiler_params=pltpu.CompilerParams(vmem_limit_bytes=24 * 2**20),
        cost_estimate=pl.CostEstimate(
            flops=30 * local_chans * BEAMS * FEEDS * 20,
            bytes_accessed=local_chans * BEAMS * FEEDS * 4,
            transcendentals=0,
        ),
        name="weights",
    )(beam_grid.T, feed_pos.T)


def split(x):
    high = x.astype(BF16)
    return high, (x - high.astype(F32)).astype(BF16)


def beams_kernel(
    w_hbm, v_ref, table_ref, flags_ref, out_ref, w_buf, sem, beam_ref, inten_ref, sum_ref, rows_ref
):
    slots = w_buf.shape[0]
    steps = BEAMS // ROWS
    size = 2 * TIME

    def fetch(i):
        return pltpu.make_async_copy(w_hbm.at[i // steps, i % steps], w_buf.at[i % slots], sem.at[i % slots])

    for i in range(slots):
        fetch(i).start()
    beam_ref[1] = jnp.zeros_like(beam_ref[1])
    sum_ref[...] = jnp.zeros_like(sum_ref)

    def detect(i):
        high, low = split(beam_ref[i % 2])
        fine = (
            jnp.dot(high, table_ref[:size], preferred_element_type=F32)
            + jnp.dot(high, table_ref[size:], preferred_element_type=F32)
            + jnp.dot(low, table_ref[:size], preferred_element_type=F32)
        )
        real, imag = fine[:, :TIME], fine[:, TIME:]
        intensity = real * real + imag * imag
        inten_ref[pl.ds(pl.multiple_of(i * ROWS, ROWS), ROWS), :] = intensity
        sum_ref[i] = jnp.sum(intensity.reshape(ROWS // 8, 8, TIME), axis=0)

    def normalize(chan):
        total = jnp.sum(sum_ref[chan * steps : (chan + 1) * steps], axis=0)
        total = jnp.broadcast_to(jnp.sum(total, axis=0, keepdims=True), (8, TIME))
        for shift in (64, 32, 16):
            total = total + pltpu.roll(total, shift, 1)
        bandpass = total[0:1] * (1.0 / (BEAMS * TOUT)) + 1e-06
        scale = flags_ref[chan : chan + 1, :] / bandpass

        def move(j, carry):
            for beam in range(2):
                x = inten_ref[pl.ds(chan * BEAMS + j * 128 + beam, 64, stride=2), :]
                rows_ref[pl.ds(j * 256 + 2 * chan + beam, 64, stride=4), :] = x * scale
            if chan == 1:
                rows = pl.ds(pl.multiple_of(j * 256, 256), 256)
                out_ref[rows, :] = rows_ref[rows, :].astype(BF16)
            return carry

        lax.fori_loop(0, BEAMS // 128, move, 0, unroll=True)

    def body(i, carry):
        fetch(i).wait()
        rhs = v_ref[:, i // steps].reshape(FEEDS, size)
        part = jnp.dot(w_buf[i % slots].reshape(2 * ROWS, FEEDS), rhs, preferred_element_type=F32)
        detect(jnp.maximum(i - 1, 0))
        beam_ref[i % 2, :, :TIME] = part[:ROWS, :TIME] - part[ROWS:, TIME:]
        beam_ref[i % 2, :, TIME:] = part[:ROWS, TIME:] + part[ROWS:, :TIME]

        @pl.when(i + slots < 2 * steps)
        def _():
            fetch(i + slots).start()

        @pl.when(i == steps)
        def _():
            normalize(0)

        return carry

    lax.fori_loop(0, 2 * steps, body, 0)
    detect(2 * steps - 1)
    normalize(1)


def dft_table():
    n = np.arange(TIME)
    same = n[:, None] // UPCHAN == n[None, :] // UPCHAN
    angle = 2 * np.pi * ((n[:, None] * n[None, :]) % UPCHAN) / UPCHAN
    cos, sin = np.cos(angle) * same / 4.0, np.sin(angle) * same / 4.0
    table = np.block([[cos, -sin], [sin, cos]]).astype(np.float32)
    high = table.astype(jnp.bfloat16)
    low = (table - high.astype(np.float32)).astype(jnp.bfloat16)
    return np.concatenate([high, low], 0)


def form_beams(w, v, flags):
    slots = 4
    vmem = pl.BlockSpec(memory_space=pltpu.VMEM)
    return pl.pallas_call(
        beams_kernel,
        in_specs=[pl.BlockSpec(memory_space=pltpu.HBM), vmem, vmem, vmem],
        out_specs=vmem,
        out_shape=jax.ShapeDtypeStruct((2 * BEAMS, TIME), BF16),
        scratch_shapes=[
            pltpu.VMEM((slots, 2, ROWS, FEEDS), BF16),
            pltpu.SemaphoreType.DMA((slots,)),
            pltpu.VMEM((2, ROWS, 2 * TIME), F32),
            pltpu.VMEM((2 * BEAMS, TIME), F32),
            pltpu.VMEM((2 * BEAMS // ROWS, 8, TIME), F32),
            pltpu.VMEM((2 * BEAMS, TIME), F32),
        ],
        compiler_params=pltpu.CompilerParams(vmem_limit_bytes=32 * 2**20),
        name="beams",
    )(pltpu.with_memory_space_constraint(w, pltpu.HBM), v, jnp.asarray(dft_table()), flags)


def finish_kernel(in_ref, power_ref, sums_ref):
    def gather_from(r):
        combo = (r >> 6) * 8 + (r & 7)
        eighth = (r >> 3) & 7
        return (eighth >> 1) * 64 + (combo >> 1) * 4 + (eighth & 1) * 2 + (combo & 1)

    def scatter_from(r):
        combo = r >> 3
        return (combo >> 3) * 64 + (r & 7) * 8 + (combo & 7)

    first, second = onehot(256, gather_from), onehot(256, scatter_from)
    lane = lax.broadcasted_iota(jnp.int32, (8, TIME), 1)
    for q in range(8):
        x = jnp.dot(first, in_ref[q * 256 : (q + 1) * 256, :], preferred_element_type=F32)
        blocks = []
        for group in range(4):
            tiles = [x[group * 64 + i * 8 : group * 64 + i * 8 + 8, :] for i in range(8)]
            for bit in (1, 2, 4):
                upper = (lane & (16 * bit)) != 0
                for i in range(8):
                    if i & bit == 0:
                        low, high = tiles[i], tiles[i | bit]
                        if bit == 4:
                            moved = pltpu.roll(jnp.where(upper, low, high), 64, 1)
                            tiles[i] = jnp.where(upper, moved, low)
                            tiles[i | bit] = jnp.where(upper, high, moved)
                            continue
                        tiles[i] = jnp.where(upper, pltpu.roll(high, 16 * bit, 1), low)
                        tiles[i | bit] = jnp.where(upper, high, pltpu.roll(low, TIME - 16 * bit, 1))
            total = sum(tiles[1:], tiles[0])
            squares = sum([t * t for t in tiles[1:]], tiles[0] * tiles[0])
            for member in range(4):
                gy = group * 4 + member
                at = (gy * 8 + q) * TIME
                sums_ref[0, :, at : at + TIME] = total[2 * member : 2 * member + 2, :]
                sums_ref[1, :, at : at + TIME] = squares[2 * member : 2 * member + 2, :]
            blocks += tiles
        y = jnp.concatenate(blocks, 0).astype(BF16)
        z = jnp.dot(second, y, preferred_element_type=F32).astype(BF16)
        for gy in range(16):
            at = (gy * 8 + q) * TIME
            for beam in range(2):
                row = gy * 16 + beam * 8
                power_ref[beam, :, at : at + TIME] = z[row : row + 8, :]


def finish(received):
    freqs = 512 * 2 * UPCHAN
    return pl.pallas_call(
        finish_kernel,
        out_shape=(
            jax.ShapeDtypeStruct((2, TOUT, freqs), BF16),
            jax.ShapeDtypeStruct((2, 2, freqs), F32),
        ),
        compiler_params=pltpu.CompilerParams(vmem_limit_bytes=24 * 2**20),
        name="finish",
    )(received)


def per_device(voltages, beam_grid, feed_pos, rfi_mask):
    inputs = lax.axis_size("gx")
    chan_dev = voltages.shape[2]
    local_chans = chan_dev // inputs
    sent = regroup(voltages)
    piece = lax.all_to_all(sent, "gx", split_axis=0, concat_axis=0, tiled=True)
    w = weights(beam_grid, feed_pos, local_chans)
    flags = rfi_mask.reshape(TOUT, local_chans, UPCHAN).transpose(1, 0, 2).astype(F32)
    piece = piece.reshape(inputs, local_chans, voltages.shape[1], 2 * TIME)
    power = form_beams(w, piece, flags.reshape(local_chans, TIME))
    power = power.reshape(512, 4, TIME)
    power = lax.all_to_all(power, ("gx", "gy"), split_axis=0, concat_axis=0, tiled=True)
    return finish(power.reshape(2048, TIME))


def solution(mesh):
    in_specs = (P(None, "gx", "gy", None), P(), P(), P(None, ("gy", "gx")))
    out_specs = (P(("gx", "gy"), None, None), P(None, ("gx", "gy"), None))
    return jax.shard_map(
        per_device, mesh=mesh, in_specs=in_specs, out_specs=out_specs, check_vma=False
    )
```

```python
import functools
import math

import jax
import jax.numpy as jnp
import numpy as np
from jax import lax
from jax.experimental import pallas as pl
from jax.experimental.pallas import tpu as pltpu
from jax.sharding import PartitionSpec as P

FEEDS = 2048
BEAMS = 1024
UPCHAN = 16
TOUT = 8
TIME = 128
F32 = jnp.float32
BF16 = jnp.bfloat16


def fit(values, degree):
    cheb = np.polynomial.Chebyshev.interpolate(values, degree, domain=[0.0, 0.25])
    return [float(c) for c in cheb.convert(kind=np.polynomial.Polynomial).coef]


COS = fit(lambda u: np.cos(2 * np.pi * np.sqrt(u)), 6)
SIN = fit(lambda u: 2 * np.pi * np.sinc(2 * np.sqrt(u)), 6)


def onehot(size, source_of):
    row = lax.broadcasted_iota(jnp.int32, (size, size), 0)
    col = lax.broadcasted_iota(jnp.int32, (size, size), 1)
    return (col == source_of(row)).astype(F32).astype(BF16)


def regroup_kernel(v_ref, out_ref, in_buf, out_buf, in_sem, out_sem):
    parts, feeds, chans, _ = v_ref.shape
    pieces = [(part, f) for f in range(0, feeds, 16) for part in range(parts)]

    def fetch(n):
        at = (pieces[n][0], pl.ds(pieces[n][1], 16))
        return pltpu.make_async_copy(v_ref.at[at], in_buf.at[at], in_sem.at[n])

    def store(n):
        at = (slice(None), pieces[n][0], pl.ds(pieces[n][1], 16))
        return pltpu.make_async_copy(out_buf.at[at], out_ref.at[at], out_sem.at[n])

    for n in range(len(pieces)):
        fetch(n).start()
    for n, (part, f) in enumerate(pieces):
        fetch(n).wait()
        for c in range(0, chans, 16):
            tile = in_buf[part, f : f + 16, c : c + 16]
            out_buf[c : c + 16, part, f : f + 16, :] = jnp.swapaxes(tile, 0, 1)
        store(n).start()
    for n in range(len(pieces)):
        store(n).wait()


def regroup(v):
    parts, feeds, chans, time = v.shape
    count = parts * feeds // 16
    return pl.pallas_call(
        regroup_kernel,
        in_specs=[pl.BlockSpec(memory_space=pltpu.HBM)],
        out_specs=pl.BlockSpec(memory_space=pltpu.HBM),
        out_shape=pltpu.HBM((chans, parts, feeds, time), BF16),
        scratch_shapes=[
            pltpu.VMEM(v.shape, BF16),
            pltpu.VMEM((chans, parts, feeds, time), BF16),
            pltpu.SemaphoreType.DMA((count,)),
            pltpu.SemaphoreType.DMA((count,)),
        ],
        compiler_params=pltpu.CompilerParams(vmem_limit_bytes=16 * 2**20),
        name="regroup",
    )(pltpu.with_memory_space_constraint(v, pltpu.HBM))


def weights_kernel(local_chans, beam_ref, feed_ref, out_ref, head_ref, turns_ref):
    device = lax.axis_index("gy") * lax.axis_size("gx") + lax.axis_index("gx")
    factor = (device * local_chans + pl.program_id(0) + 400) % 4096
    bm = beam_ref.shape[1]

    def rows_of(ref):
        row = lax.broadcasted_iota(jnp.int32, (16, ref.shape[1]), 0)
        return row, jnp.where(row < 2, ref[0:1, :], ref[1:2, :])

    row, grid = rows_of(beam_ref)
    part = (grid * factor) & 4095
    left = jnp.where((row & 1) == 0, part & 4032, part & 63)
    left = jnp.where(row < 4, left, 0).astype(F32).astype(BF16)
    right = rows_of(feed_ref)[1].astype(F32).astype(BF16)
    turns_ref[...] = lax.dot_general(
        left, right, (((0,), (0,)), ((), ())), preferred_element_type=F32
    )
    scale = 1.0 / math.sqrt(FEEDS)
    width = 512

    def chunk(i, carry):
        r0 = pl.multiple_of(i * 16, 16)
        for c0 in range(0, FEEDS, width):
            t = turns_ref[pl.ds(r0, 16), c0 : c0 + width] * (1.0 / 4096.0)
            r = t - jnp.round(t)
            u = r * r
            c = COS[-1] * scale
            for coef in COS[-2::-1]:
                c = c * u + coef * scale
            s = -SIN[-1] * scale
            for coef in SIN[-2::-1]:
                s = s * u - coef * scale
            out_ref[0, pl.ds(r0, 16), c0 : c0 + width] = c.astype(BF16)
            out_ref[0, pl.ds(r0, 16), FEEDS + c0 : FEEDS + c0 + width] = (s * r).astype(BF16)
        return carry

    lax.fori_loop(0, bm // 16, chunk, 0)

    @pl.when((pl.program_id(0) == 0) & (pl.program_id(1) == 0))
    def _():
        head_ref[...] = out_ref[0]


def weights(beam_grid, feed_pos, local_chans):
    bm = 128
    return pl.pallas_call(
        functools.partial(weights_kernel, local_chans),
        grid=(local_chans, BEAMS // bm),
        in_specs=[
            pl.BlockSpec((2, bm), lambda c, m: (0, m)),
            pl.BlockSpec((2, FEEDS), lambda c, m: (0, 0)),
        ],
        out_specs=(
            pl.BlockSpec((1, bm, 2 * FEEDS), lambda c, m: (c, m, 0)),
            pl.BlockSpec((bm, 2 * FEEDS), lambda c, m: (0, 0)),
        ),
        out_shape=(
            pltpu.HBM((local_chans, BEAMS, 2 * FEEDS), BF16),
            jax.ShapeDtypeStruct((bm, 2 * FEEDS), BF16),
        ),
        scratch_shapes=[pltpu.VMEM((bm, FEEDS), F32)],
        compiler_params=pltpu.CompilerParams(vmem_limit_bytes=24 * 2**20),
        cost_estimate=pl.CostEstimate(
            flops=30 * local_chans * BEAMS * FEEDS * 20,
            bytes_accessed=local_chans * BEAMS * FEEDS * 4,
            transcendentals=0,
        ),
        name="weights",
    )(beam_grid.T, feed_pos.T)


def split(x):
    high = x.astype(BF16)
    return high, (x - high.astype(F32)).astype(BF16)


def beams_kernel(
    w_hbm, head_ref, v_ref, table_ref, flags_ref, out_ref, w_buf, sem, rhs_ref, beam_ref, inten_ref, rows_ref, sum_ref
):
    slots, bm, _ = w_buf.shape
    steps = BEAMS // bm
    size = 2 * TIME

    def fetch(i):
        rows = pl.ds(pl.multiple_of(i % steps * bm, bm), bm)
        return pltpu.make_async_copy(w_hbm.at[i // steps, rows], w_buf.at[i % slots], sem.at[i % slots])

    kept = head_ref.shape[0]
    rest = pl.ds(kept, bm - kept)
    pltpu.make_async_copy(w_hbm.at[0, rest], w_buf.at[0, rest], sem.at[0]).start()
    pltpu.make_async_copy(head_ref, w_buf.at[0, pl.ds(0, kept)], sem.at[0]).start()
    for i in range(1, slots):
        fetch(i).start()
    for chan in range(2):
        real = v_ref[:, chan, 0].reshape(FEEDS, TIME)
        imag = v_ref[:, chan, 1].reshape(FEEDS, TIME)
        rhs_ref[chan, :FEEDS, :TIME] = real
        rhs_ref[chan, :FEEDS, TIME:] = imag
        rhs_ref[chan, FEEDS:, :TIME] = -imag
        rhs_ref[chan, FEEDS:, TIME:] = real
    beam_ref[1] = jnp.zeros_like(beam_ref[1])

    def detect(i):
        high, low = split(beam_ref[i % 2])
        fine = (
            jnp.dot(high, table_ref[:size], preferred_element_type=F32)
            + jnp.dot(high, table_ref[size:], preferred_element_type=F32)
            + jnp.dot(low, table_ref[:size], preferred_element_type=F32)
        )
        real, imag = fine[:, :TIME], fine[:, TIME:]
        rows = pl.ds(pl.multiple_of(i % steps * bm, bm), bm)
        x = real * real + imag * imag
        inten_ref[i // steps, rows, :] = x
        sum_ref[i] = jnp.sum(x.reshape(bm // 8, 8, TIME), axis=0)

    def normalize(chan):
        total = jnp.sum(sum_ref[chan * steps : (chan + 1) * steps], axis=0)
        total = jnp.broadcast_to(jnp.sum(total, axis=0, keepdims=True), (8, TIME))
        for shift in (64, 32, 16):
            total = total + pltpu.roll(total, shift, 1)
        bandpass = total[0:1] * (1.0 / (BEAMS * TOUT)) + 1e-06
        scale = flags_ref[chan : chan + 1, :] / bandpass

        def move(j, carry):
            for beam in range(2):
                x = inten_ref[chan, pl.ds(j * 128 + beam, 64, stride=2), :]
                rows_ref[pl.ds(j * 256 + 2 * chan + beam, 64, stride=4), :] = x * scale
            if chan == 1:
                rows = pl.ds(pl.multiple_of(j * 256, 256), 256)
                out_ref[rows, :] = rows_ref[rows, :].astype(BF16)
            return carry

        lax.fori_loop(0, BEAMS // 128, move, 0, unroll=True)

    def body(i, carry):
        fetch(i).wait()
        beam = jnp.dot(w_buf[i % slots], rhs_ref[i // steps], preferred_element_type=F32)
        detect(jnp.maximum(i - 1, 0))
        beam_ref[i % 2] = beam

        @pl.when(i + slots < 2 * steps)
        def _():
            fetch(i + slots).start()

        @pl.when(i == steps)
        def _():
            normalize(0)

        return carry

    lax.fori_loop(0, 2 * steps, body, 0)
    detect(2 * steps - 1)
    normalize(1)


def dft_table():
    n = np.arange(TIME)
    same = n[:, None] // UPCHAN == n[None, :] // UPCHAN
    angle = 2 * np.pi * ((n[:, None] * n[None, :]) % UPCHAN) / UPCHAN
    cos, sin = np.cos(angle) * same / 4.0, np.sin(angle) * same / 4.0
    table = np.block([[cos, -sin], [sin, cos]]).astype(np.float32)
    high = table.astype(jnp.bfloat16)
    low = (table - high.astype(np.float32)).astype(jnp.bfloat16)
    return np.concatenate([high, low], 0)


def form_beams(w, head, v, flags):
    bm, slots = 256, 4
    vmem = pl.BlockSpec(memory_space=pltpu.VMEM)
    return pl.pallas_call(
        beams_kernel,
        in_specs=[pl.BlockSpec(memory_space=pltpu.HBM), vmem, vmem, vmem, vmem],
        out_specs=vmem,
        out_shape=jax.ShapeDtypeStruct((2 * BEAMS, TIME), BF16),
        scratch_shapes=[
            pltpu.VMEM((slots, bm, 2 * FEEDS), BF16),
            pltpu.SemaphoreType.DMA((slots,)),
            pltpu.VMEM((2, 2 * FEEDS, 2 * TIME), BF16),
            pltpu.VMEM((2, bm, 2 * TIME), F32),
            pltpu.VMEM((2, BEAMS, TIME), F32),
            pltpu.VMEM((2 * BEAMS, TIME), F32),
            pltpu.VMEM((2 * BEAMS // bm, 8, TIME), F32),
        ],
        compiler_params=pltpu.CompilerParams(vmem_limit_bytes=32 * 2**20),
        name="beams",
    )(pltpu.with_memory_space_constraint(w, pltpu.HBM), head, v, jnp.asarray(dft_table()), flags)


def finish_kernel(in_ref, power_ref, sums_ref):
    def gather_from(r):
        combo = (r >> 6) * 8 + (r & 7)
        eighth = (r >> 3) & 7
        return (eighth >> 1) * 64 + (combo >> 1) * 4 + (eighth & 1) * 2 + (combo & 1)

    def scatter_from(r):
        combo = r >> 3
        return (combo >> 3) * 64 + (r & 7) * 8 + (combo & 7)

    first, second = onehot(256, gather_from), onehot(256, scatter_from)
    lane = lax.broadcasted_iota(jnp.int32, (8, TIME), 1)
    for q in range(8):
        x = jnp.dot(first, in_ref[q * 256 : (q + 1) * 256, :], preferred_element_type=F32)
        blocks = []
        for group in range(4):
            tiles = [x[group * 64 + i * 8 : group * 64 + i * 8 + 8, :] for i in range(8)]
            for bit in (1, 2, 4):
                upper = (lane & (16 * bit)) != 0
                for i in range(8):
                    if i & bit == 0:
                        low, high = tiles[i], tiles[i | bit]
                        tiles[i] = jnp.where(upper, pltpu.roll(high, 16 * bit, 1), low)
                        tiles[i | bit] = jnp.where(upper, high, pltpu.roll(low, TIME - 16 * bit, 1))
            total = sum(tiles[1:], tiles[0])
            squares = sum([t * t for t in tiles[1:]], tiles[0] * tiles[0])
            for member in range(4):
                gy = group * 4 + member
                at = (gy * 8 + q) * TIME
                sums_ref[0, :, at : at + TIME] = total[2 * member : 2 * member + 2, :]
                sums_ref[1, :, at : at + TIME] = squares[2 * member : 2 * member + 2, :]
            blocks += tiles
        y = jnp.concatenate(blocks, 0).astype(BF16)
        z = jnp.dot(second, y, preferred_element_type=F32).astype(BF16)
        for gy in range(16):
            at = (gy * 8 + q) * TIME
            for beam in range(2):
                row = gy * 16 + beam * 8
                power_ref[beam, :, at : at + TIME] = z[row : row + 8, :]


def finish(received):
    freqs = 512 * 2 * UPCHAN
    return pl.pallas_call(
        finish_kernel,
        out_shape=(
            jax.ShapeDtypeStruct((2, TOUT, freqs), BF16),
            jax.ShapeDtypeStruct((2, 2, freqs), F32),
        ),
        compiler_params=pltpu.CompilerParams(vmem_limit_bytes=24 * 2**20),
        name="finish",
    )(received)


def per_device(voltages, beam_grid, feed_pos, rfi_mask):
    inputs = lax.axis_size("gx")
    chan_dev = voltages.shape[2]
    local_chans = chan_dev // inputs
    sent = regroup(voltages)
    piece = lax.all_to_all(sent, "gx", split_axis=0, concat_axis=0, tiled=True)
    w, head = weights(beam_grid, feed_pos, local_chans)
    flags = rfi_mask.reshape(TOUT, local_chans, UPCHAN).transpose(1, 0, 2).astype(F32)
    piece = piece.reshape(inputs, local_chans, 2, voltages.shape[1], TIME)
    power = form_beams(w, head, piece, flags.reshape(local_chans, TIME))
    power = power.reshape(512, 4, TIME)
    power = lax.all_to_all(power, ("gx", "gy"), split_axis=0, concat_axis=0, tiled=True)
    return finish(power.reshape(2048, TIME))


def solution(mesh):
    in_specs = (P(None, "gx", "gy", None), P(), P(), P(None, ("gy", "gx")))
    out_specs = (P(("gx", "gy"), None, None), P(None, ("gx", "gy"), None))
    return jax.shard_map(
        per_device, mesh=mesh, in_specs=in_specs, out_specs=out_specs, check_vma=False
    )
```

```python
import functools
import math

import jax
import jax.numpy as jnp
import numpy as np
from jax import lax
from jax.experimental import pallas as pl
from jax.experimental.pallas import tpu as pltpu
from jax.sharding import PartitionSpec as P

FEEDS = 2048
BEAMS = 1024
UPCHAN = 16
TOUT = 8
TIME = 128
ROWS = 256
F32 = jnp.float32
BF16 = jnp.bfloat16


def fit(values, degree):
    cheb = np.polynomial.Chebyshev.interpolate(values, degree, domain=[0.0, 0.25])
    return [float(c) for c in cheb.convert(kind=np.polynomial.Polynomial).coef]


COS = fit(lambda u: np.cos(2 * np.pi * np.sqrt(u)), 6)
SIN = fit(lambda u: 2 * np.pi * np.sinc(2 * np.sqrt(u)), 6)


def onehot(size, source_of):
    row = lax.broadcasted_iota(jnp.int32, (size, size), 0)
    col = lax.broadcasted_iota(jnp.int32, (size, size), 1)
    return (col == source_of(row)).astype(F32).astype(BF16)


def regroup_kernel(v_ref, out_ref, in_buf, out_buf, in_sem, out_sem):
    parts, feeds, chans, time = v_ref.shape
    pieces = [(part, f) for f in range(0, feeds, 16) for part in range(parts)]

    def fetch(n):
        at = (pieces[n][0], pl.ds(pieces[n][1], 16))
        return pltpu.make_async_copy(v_ref.at[at], in_buf.at[at], in_sem.at[n])

    def store(n):
        at = (slice(None), pl.ds(n * 16, 16))
        return pltpu.make_async_copy(out_buf.at[at], out_ref.at[at], out_sem.at[n])

    for n in range(len(pieces)):
        fetch(n).start()
    for n, (part, f) in enumerate(pieces):
        fetch(n).wait()
        for c in range(0, chans, 16):
            tile = jnp.swapaxes(in_buf[part, f : f + 16, c : c + 16], 0, 1)
            out_buf[c : c + 16, f : f + 16, part * time : (part + 1) * time] = tile
        if part == parts - 1:
            store(f // 16).start()
    for n in range(feeds // 16):
        store(n).wait()


def regroup(v):
    parts, feeds, chans, time = v.shape
    shape = (chans, feeds, parts * time)
    return pl.pallas_call(
        regroup_kernel,
        in_specs=[pl.BlockSpec(memory_space=pltpu.HBM)],
        out_specs=pl.BlockSpec(memory_space=pltpu.HBM),
        out_shape=pltpu.HBM(shape, BF16),
        scratch_shapes=[
            pltpu.VMEM(v.shape, BF16),
            pltpu.VMEM(shape, BF16),
            pltpu.SemaphoreType.DMA((parts * feeds // 16,)),
            pltpu.SemaphoreType.DMA((feeds // 16,)),
        ],
        compiler_params=pltpu.CompilerParams(vmem_limit_bytes=16 * 2**20),
        name="regroup",
    )(pltpu.with_memory_space_constraint(v, pltpu.HBM))


def weights_kernel(local_chans, beam_ref, feed_ref, out_ref, head_ref, turns_ref):
    device = lax.axis_index("gy") * lax.axis_size("gx") + lax.axis_index("gx")
    factor = (device * local_chans + pl.program_id(0) + 400) % 4096
    bm = beam_ref.shape[1]

    def rows_of(ref):
        row = lax.broadcasted_iota(jnp.int32, (16, ref.shape[1]), 0)
        return row, jnp.where(row < 2, ref[0:1, :], ref[1:2, :])

    row, grid = rows_of(beam_ref)
    part = (grid * factor) & 4095
    left = jnp.where((row & 1) == 0, part & 4032, part & 63)
    left = jnp.where(row < 4, left, 0).astype(F32).astype(BF16)
    right = rows_of(feed_ref)[1].astype(F32).astype(BF16)
    turns_ref[...] = lax.dot_general(
        left, right, (((0,), (0,)), ((), ())), preferred_element_type=F32
    )
    scale = 1.0 / math.sqrt(FEEDS)
    width = 512

    def chunk(i, carry):
        r0 = pl.multiple_of(i * 16, 16)
        for c0 in range(0, FEEDS, width):
            t = turns_ref[pl.ds(r0, 16), c0 : c0 + width] * (1.0 / 4096.0)
            r = t - jnp.round(t)
            u = r * r
            c = COS[-1] * scale
            for coef in COS[-2::-1]:
                c = c * u + coef * scale
            s = -SIN[-1] * scale
            for coef in SIN[-2::-1]:
                s = s * u - coef * scale
            out_ref[0, 0, 0, pl.ds(r0, 16), c0 : c0 + width] = c.astype(BF16)
            out_ref[0, 0, 1, pl.ds(r0, 16), c0 : c0 + width] = (s * r).astype(BF16)
        return carry

    lax.fori_loop(0, bm // 16, chunk, 0)

    @pl.when((pl.program_id(0) == 0) & (pl.program_id(1) == 0))
    def _():
        head_ref[...] = out_ref[0, 0]


def weights(beam_grid, feed_pos, local_chans):
    bm = 128
    per = ROWS // bm
    return pl.pallas_call(
        functools.partial(weights_kernel, local_chans),
        grid=(local_chans, BEAMS // bm),
        in_specs=[
            pl.BlockSpec((2, bm), lambda c, m: (0, m)),
            pl.BlockSpec((2, FEEDS), lambda c, m: (0, 0)),
        ],
        out_specs=(
            pl.BlockSpec((1, 1, 2, bm, FEEDS), lambda c, m: (c, m // per, 0, m % per, 0)),
            pl.BlockSpec((2, bm, FEEDS), lambda c, m: (0, 0, 0)),
        ),
        out_shape=(
            pltpu.HBM((local_chans, BEAMS // ROWS, 2, ROWS, FEEDS), BF16),
            jax.ShapeDtypeStruct((2, bm, FEEDS), BF16),
        ),
        scratch_shapes=[pltpu.VMEM((bm, FEEDS), F32)],
        compiler_params=pltpu.CompilerParams(vmem_limit_bytes=24 * 2**20),
        cost_estimate=pl.CostEstimate(
            flops=30 * local_chans * BEAMS * FEEDS * 20,
            bytes_accessed=local_chans * BEAMS * FEEDS * 4,
            transcendentals=0,
        ),
        name="weights",
    )(beam_grid.T, feed_pos.T)


def split(x):
    high = x.astype(BF16)
    return high, (x - high.astype(F32)).astype(BF16)


def beams_kernel(
    w_hbm, head_ref, v_ref, table_ref, flags_ref, out_ref, w_buf, sem, beam_ref, inten_ref, sum_ref, rows_ref
):
    slots = w_buf.shape[0]
    steps = BEAMS // ROWS
    size = 2 * TIME

    def fetch(i):
        return pltpu.make_async_copy(w_hbm.at[i // steps, i % steps], w_buf.at[i % slots], sem.at[i % slots])

    kept = head_ref.shape[1]
    for part in range(2):
        rest = pl.ds(kept, ROWS - kept)
        pltpu.make_async_copy(w_hbm.at[0, 0, part, rest], w_buf.at[0, part, rest], sem.at[0]).start()
        first = w_buf.at[0, part, pl.ds(0, kept)]
        pltpu.make_async_copy(head_ref.at[part], first, sem.at[0]).start()
    for i in range(1, slots):
        fetch(i).start()
    beam_ref[1] = jnp.zeros_like(beam_ref[1])
    sum_ref[...] = jnp.zeros_like(sum_ref)

    def detect(i):
        high, low = split(beam_ref[i % 2])
        fine = (
            jnp.dot(high, table_ref[:size], preferred_element_type=F32)
            + jnp.dot(high, table_ref[size:], preferred_element_type=F32)
            + jnp.dot(low, table_ref[:size], preferred_element_type=F32)
        )
        real, imag = fine[:, :TIME], fine[:, TIME:]
        intensity = real * real + imag * imag
        inten_ref[pl.ds(pl.multiple_of(i * ROWS, ROWS), ROWS), :] = intensity
        sum_ref[i] = jnp.sum(intensity.reshape(ROWS // 8, 8, TIME), axis=0)

    def normalize(chan):
        total = jnp.sum(sum_ref[chan * steps : (chan + 1) * steps], axis=0)
        total = jnp.broadcast_to(jnp.sum(total, axis=0, keepdims=True), (8, TIME))
        for shift in (64, 32, 16):
            total = total + pltpu.roll(total, shift, 1)
        bandpass = total[0:1] * (1.0 / (BEAMS * TOUT)) + 1e-06
        scale = flags_ref[chan : chan + 1, :] / bandpass

        def move(j, carry):
            for beam in range(2):
                x = inten_ref[pl.ds(chan * BEAMS + j * 128 + beam, 64, stride=2), :]
                rows_ref[pl.ds(j * 256 + 2 * chan + beam, 64, stride=4), :] = x * scale
            if chan == 1:
                rows = pl.ds(pl.multiple_of(j * 256, 256), 256)
                out_ref[rows, :] = rows_ref[rows, :].astype(BF16)
            return carry

        lax.fori_loop(0, BEAMS // 128, move, 0, unroll=True)

    def body(i, carry):
        fetch(i).wait()
        rhs = v_ref[:, i // steps].reshape(FEEDS, size)
        part = jnp.dot(w_buf[i % slots].reshape(2 * ROWS, FEEDS), rhs, preferred_element_type=F32)
        detect(jnp.maximum(i - 1, 0))
        beam_ref[i % 2, :, :TIME] = part[:ROWS, :TIME] - part[ROWS:, TIME:]
        beam_ref[i % 2, :, TIME:] = part[:ROWS, TIME:] + part[ROWS:, :TIME]

        @pl.when(i + slots < 2 * steps)
        def _():
            fetch(i + slots).start()

        @pl.when(i == steps)
        def _():
            normalize(0)

        return carry

    lax.fori_loop(0, 2 * steps, body, 0)
    detect(2 * steps - 1)
    normalize(1)


def dft_table():
    n = np.arange(TIME)
    same = n[:, None] // UPCHAN == n[None, :] // UPCHAN
    angle = 2 * np.pi * ((n[:, None] * n[None, :]) % UPCHAN) / UPCHAN
    cos, sin = np.cos(angle) * same / 4.0, np.sin(angle) * same / 4.0
    table = np.block([[cos, -sin], [sin, cos]]).astype(np.float32)
    high = table.astype(jnp.bfloat16)
    low = (table - high.astype(np.float32)).astype(jnp.bfloat16)
    return np.concatenate([high, low], 0)


def form_beams(w, head, v, flags):
    slots = 4
    vmem = pl.BlockSpec(memory_space=pltpu.VMEM)
    return pl.pallas_call(
        beams_kernel,
        in_specs=[pl.BlockSpec(memory_space=pltpu.HBM), vmem, vmem, vmem, vmem],
        out_specs=vmem,
        out_shape=jax.ShapeDtypeStruct((2 * BEAMS, TIME), BF16),
        scratch_shapes=[
            pltpu.VMEM((slots, 2, ROWS, FEEDS), BF16),
            pltpu.SemaphoreType.DMA((slots,)),
            pltpu.VMEM((2, ROWS, 2 * TIME), F32),
            pltpu.VMEM((2 * BEAMS, TIME), F32),
            pltpu.VMEM((2 * BEAMS // ROWS, 8, TIME), F32),
            pltpu.VMEM((2 * BEAMS, TIME), F32),
        ],
        compiler_params=pltpu.CompilerParams(vmem_limit_bytes=32 * 2**20),
        name="beams",
    )(pltpu.with_memory_space_constraint(w, pltpu.HBM), head, v, jnp.asarray(dft_table()), flags)


def finish_kernel(in_ref, power_ref, sums_ref):
    def gather_from(r):
        combo = (r >> 6) * 8 + (r & 7)
        eighth = (r >> 3) & 7
        return (eighth >> 1) * 64 + (combo >> 1) * 4 + (eighth & 1) * 2 + (combo & 1)

    def scatter_from(r):
        combo = r >> 3
        return (combo >> 3) * 64 + (r & 7) * 8 + (combo & 7)

    first, second = onehot(256, gather_from), onehot(256, scatter_from)
    lane = lax.broadcasted_iota(jnp.int32, (8, TIME), 1)
    for q in range(8):
        x = jnp.dot(first, in_ref[q * 256 : (q + 1) * 256, :], preferred_element_type=F32)
        blocks = []
        for group in range(4):
            tiles = [x[group * 64 + i * 8 : group * 64 + i * 8 + 8, :] for i in range(8)]
            for bit in (1, 2, 4):
                upper = (lane & (16 * bit)) != 0
                for i in range(8):
                    if i & bit == 0:
                        low, high = tiles[i], tiles[i | bit]
                        if bit == 4:
                            moved = pltpu.roll(jnp.where(upper, low, high), 64, 1)
                            tiles[i] = jnp.where(upper, moved, low)
                            tiles[i | bit] = jnp.where(upper, high, moved)
                            continue
                        tiles[i] = jnp.where(upper, pltpu.roll(high, 16 * bit, 1), low)
                        tiles[i | bit] = jnp.where(upper, high, pltpu.roll(low, TIME - 16 * bit, 1))
            total = sum(tiles[1:], tiles[0])
            squares = sum([t * t for t in tiles[1:]], tiles[0] * tiles[0])
            for member in range(4):
                gy = group * 4 + member
                at = (gy * 8 + q) * TIME
                sums_ref[0, :, at : at + TIME] = total[2 * member : 2 * member + 2, :]
                sums_ref[1, :, at : at + TIME] = squares[2 * member : 2 * member + 2, :]
            blocks += tiles
        y = jnp.concatenate(blocks, 0).astype(BF16)
        z = jnp.dot(second, y, preferred_element_type=F32).astype(BF16)
        for gy in range(16):
            at = (gy * 8 + q) * TIME
            for beam in range(2):
                row = gy * 16 + beam * 8
                power_ref[beam, :, at : at + TIME] = z[row : row + 8, :]


def finish(received):
    freqs = 512 * 2 * UPCHAN
    return pl.pallas_call(
        finish_kernel,
        out_shape=(
            jax.ShapeDtypeStruct((2, TOUT, freqs), BF16),
            jax.ShapeDtypeStruct((2, 2, freqs), F32),
        ),
        compiler_params=pltpu.CompilerParams(vmem_limit_bytes=24 * 2**20),
        name="finish",
    )(received)


def per_device(voltages, beam_grid, feed_pos, rfi_mask):
    inputs = lax.axis_size("gx")
    chan_dev = voltages.shape[2]
    local_chans = chan_dev // inputs
    sent = regroup(voltages)
    piece = lax.all_to_all(sent, "gx", split_axis=0, concat_axis=0, tiled=True)
    w, head = weights(beam_grid, feed_pos, local_chans)
    flags = rfi_mask.reshape(TOUT, local_chans, UPCHAN).transpose(1, 0, 2).astype(F32)
    piece = piece.reshape(inputs, local_chans, voltages.shape[1], 2 * TIME)
    power = form_beams(w, head, piece, flags.reshape(local_chans, TIME))
    power = power.reshape(512, 4, TIME)
    power = lax.all_to_all(power, ("gx", "gy"), split_axis=0, concat_axis=0, tiled=True)
    return finish(power.reshape(2048, TIME))


def solution(mesh):
    in_specs = (P(None, "gx", "gy", None), P(), P(), P(None, ("gy", "gx")))
    out_specs = (P(("gx", "gy"), None, None), P(None, ("gx", "gy"), None))
    return jax.shard_map(
        per_device, mesh=mesh, in_specs=in_specs, out_specs=out_specs, check_vma=False
    )
```

```python
import functools
import math

import jax
import jax.numpy as jnp
import numpy as np
from jax import lax
from jax.experimental import pallas as pl
from jax.experimental.pallas import tpu as pltpu
from jax.sharding import PartitionSpec as P

FEEDS = 2048
BEAMS = 1024
UPCHAN = 16
TOUT = 8
TIME = 128
ROWS = 256
F32 = jnp.float32
BF16 = jnp.bfloat16


def fit(values, degree):
    cheb = np.polynomial.Chebyshev.interpolate(values, degree, domain=[0.0, 0.25])
    return [float(c) for c in cheb.convert(kind=np.polynomial.Polynomial).coef]


COS = fit(lambda u: np.cos(2 * np.pi * np.sqrt(u)), 6)
SIN = fit(lambda u: 2 * np.pi * np.sinc(2 * np.sqrt(u)), 6)


def onehot(size, source_of):
    row = lax.broadcasted_iota(jnp.int32, (size, size), 0)
    col = lax.broadcasted_iota(jnp.int32, (size, size), 1)
    return (col == source_of(row)).astype(F32).astype(BF16)


def regroup_kernel(v_ref, out_ref, in_buf, out_buf, in_sem, out_sem):
    parts, feeds, chans, time = v_ref.shape
    pieces = [(part, f) for f in range(0, feeds, 16) for part in range(parts)]

    def fetch(n):
        at = (pieces[n][0], pl.ds(pieces[n][1], 16))
        return pltpu.make_async_copy(v_ref.at[at], in_buf.at[at], in_sem.at[n])

    def store(n):
        at = (slice(None), pl.ds(n * 16, 16))
        return pltpu.make_async_copy(out_buf.at[at], out_ref.at[at], out_sem.at[n])

    for n in range(len(pieces)):
        fetch(n).start()
    for n, (part, f) in enumerate(pieces):
        fetch(n).wait()
        for c in range(0, chans, 16):
            tile = jnp.swapaxes(in_buf[part, f : f + 16, c : c + 16], 0, 1)
            out_buf[c : c + 16, f : f + 16, part * time : (part + 1) * time] = tile
        if part == parts - 1:
            store(f // 16).start()
    for n in range(feeds // 16):
        store(n).wait()


def regroup(v):
    parts, feeds, chans, time = v.shape
    shape = (chans, feeds, parts * time)
    return pl.pallas_call(
        regroup_kernel,
        in_specs=[pl.BlockSpec(memory_space=pltpu.HBM)],
        out_specs=pl.BlockSpec(memory_space=pltpu.HBM),
        out_shape=pltpu.HBM(shape, BF16),
        scratch_shapes=[
            pltpu.VMEM(v.shape, BF16),
            pltpu.VMEM(shape, BF16),
            pltpu.SemaphoreType.DMA((parts * feeds // 16,)),
            pltpu.SemaphoreType.DMA((feeds // 16,)),
        ],
        compiler_params=pltpu.CompilerParams(vmem_limit_bytes=16 * 2**20),
        name="regroup",
    )(pltpu.with_memory_space_constraint(v, pltpu.HBM))


def weights_kernel(local_chans, beam_ref, feed_ref, out_ref, head_ref, turns_ref):
    device = lax.axis_index("gy") * lax.axis_size("gx") + lax.axis_index("gx")
    factor = (device * local_chans + pl.program_id(0) + 400) % 4096
    bm = beam_ref.shape[1]

    def rows_of(ref):
        row = lax.broadcasted_iota(jnp.int32, (16, ref.shape[1]), 0)
        return row, jnp.where(row < 2, ref[0:1, :], ref[1:2, :])

    row, grid = rows_of(beam_ref)
    part = (grid * factor) & 4095
    left = jnp.where((row & 1) == 0, part & 4032, part & 63)
    left = jnp.where(row < 4, left, 0).astype(F32).astype(BF16)
    right = rows_of(feed_ref)[1].astype(F32).astype(BF16)
    turns_ref[...] = lax.dot_general(
        left, right, (((0,), (0,)), ((), ())), preferred_element_type=F32
    )
    scale = 1.0 / math.sqrt(FEEDS)
    width = 512

    def chunk(i, carry):
        r0 = pl.multiple_of(i * 16, 16)
        for c0 in range(0, FEEDS, width):
            t = turns_ref[pl.ds(r0, 16), c0 : c0 + width] * (1.0 / 4096.0)
            r = t - jnp.round(t)
            u = r * r
            c = COS[-1] * scale
            for coef in COS[-2::-1]:
                c = c * u + coef * scale
            s = -SIN[-1] * scale
            for coef in SIN[-2::-1]:
                s = s * u - coef * scale
            out_ref[0, 0, 0, pl.ds(r0, 16), c0 : c0 + width] = c.astype(BF16)
            out_ref[0, 0, 1, pl.ds(r0, 16), c0 : c0 + width] = (s * r).astype(BF16)
        return carry

    lax.fori_loop(0, bm // 16, chunk, 0)

    @pl.when((pl.program_id(0) == 0) & (pl.program_id(1) == 0))
    def _():
        head_ref[...] = out_ref[0, 0]


def weights(beam_grid, feed_pos, local_chans):
    bm = 128
    per = ROWS // bm
    return pl.pallas_call(
        functools.partial(weights_kernel, local_chans),
        grid=(local_chans, BEAMS // bm),
        in_specs=[
            pl.BlockSpec((2, bm), lambda c, m: (0, m)),
            pl.BlockSpec((2, FEEDS), lambda c, m: (0, 0)),
        ],
        out_specs=(
            pl.BlockSpec((1, 1, 2, bm, FEEDS), lambda c, m: (c, m // per, 0, m % per, 0)),
            pl.BlockSpec((2, bm, FEEDS), lambda c, m: (0, 0, 0)),
        ),
        out_shape=(
            pltpu.HBM((local_chans, BEAMS // ROWS, 2, ROWS, FEEDS), BF16),
            jax.ShapeDtypeStruct((2, bm, FEEDS), BF16),
        ),
        scratch_shapes=[pltpu.VMEM((bm, FEEDS), F32)],
        compiler_params=pltpu.CompilerParams(vmem_limit_bytes=24 * 2**20),
        cost_estimate=pl.CostEstimate(
            flops=30 * local_chans * BEAMS * FEEDS * 20,
            bytes_accessed=local_chans * BEAMS * FEEDS * 4,
            transcendentals=0,
        ),
        name="weights",
    )(beam_grid.T, feed_pos.T)


def split(x):
    high = x.astype(BF16)
    return high, (x - high.astype(F32)).astype(BF16)


def beams_kernel(
    w_hbm, head_ref, v_ref, table_ref, flags_ref, out_ref, w_buf, sem, beam_ref, inten_ref, sum_ref, rows_ref
):
    slots = w_buf.shape[0]
    steps = BEAMS // ROWS
    size = 2 * TIME

    def fetch(i):
        return pltpu.make_async_copy(w_hbm.at[i // steps, i % steps], w_buf.at[i % slots], sem.at[i % slots])

    kept = head_ref.shape[1]
    for part in range(2):
        for row in range(kept, ROWS, 32):
            at = (0, part, pl.ds(row, 32))
            pltpu.make_async_copy(w_hbm.at[0].at[at], w_buf.at[at], sem.at[0]).start()
        first = w_buf.at[0, part, pl.ds(0, kept)]
        pltpu.make_async_copy(head_ref.at[part], first, sem.at[0]).start()
    for i in range(1, slots):
        fetch(i).start()
    beam_ref[1] = jnp.zeros_like(beam_ref[1])
    sum_ref[...] = jnp.zeros_like(sum_ref)

    def detect(i):
        high, low = split(beam_ref[i % 2])
        fine = (
            jnp.dot(high, table_ref[:size], preferred_element_type=F32)
            + jnp.dot(high, table_ref[size:], preferred_element_type=F32)
            + jnp.dot(low, table_ref[:size], preferred_element_type=F32)
        )
        real, imag = fine[:, :TIME], fine[:, TIME:]
        intensity = real * real + imag * imag
        inten_ref[pl.ds(pl.multiple_of(i * ROWS, ROWS), ROWS), :] = intensity
        sum_ref[i] = jnp.sum(intensity.reshape(ROWS // 8, 8, TIME), axis=0)

    def normalize(chan):
        total = jnp.sum(sum_ref[chan * steps : (chan + 1) * steps], axis=0)
        total = jnp.broadcast_to(jnp.sum(total, axis=0, keepdims=True), (8, TIME))
        for shift in (64, 32, 16):
            total = total + pltpu.roll(total, shift, 1)
        bandpass = total[0:1] * (1.0 / (BEAMS * TOUT)) + 1e-06
        scale = flags_ref[chan : chan + 1, :] / bandpass

        def move(j, carry):
            for beam in range(2):
                x = inten_ref[pl.ds(chan * BEAMS + j * 128 + beam, 64, stride=2), :]
                rows_ref[pl.ds(j * 256 + 2 * chan + beam, 64, stride=4), :] = x * scale
            if chan == 1:
                rows = pl.ds(pl.multiple_of(j * 256, 256), 256)
                out_ref[rows, :] = rows_ref[rows, :].astype(BF16)
            return carry

        lax.fori_loop(0, BEAMS // 128, move, 0, unroll=True)

    def body(i, carry):
        fetch(i).wait()
        rhs = v_ref[:, i // steps].reshape(FEEDS, size)
        part = jnp.dot(w_buf[i % slots].reshape(2 * ROWS, FEEDS), rhs, preferred_element_type=F32)
        detect(jnp.maximum(i - 1, 0))
        beam_ref[i % 2, :, :TIME] = part[:ROWS, :TIME] - part[ROWS:, TIME:]
        beam_ref[i % 2, :, TIME:] = part[:ROWS, TIME:] + part[ROWS:, :TIME]

        @pl.when(i + slots < 2 * steps)
        def _():
            fetch(i + slots).start()

        @pl.when(i == steps)
        def _():
            normalize(0)

        return carry

    lax.fori_loop(0, 2 * steps, body, 0)
    detect(2 * steps - 1)
    normalize(1)


def dft_table():
    n = np.arange(TIME)
    same = n[:, None] // UPCHAN == n[None, :] // UPCHAN
    angle = 2 * np.pi * ((n[:, None] * n[None, :]) % UPCHAN) / UPCHAN
    cos, sin = np.cos(angle) * same / 4.0, np.sin(angle) * same / 4.0
    table = np.block([[cos, -sin], [sin, cos]]).astype(np.float32)
    high = table.astype(jnp.bfloat16)
    low = (table - high.astype(np.float32)).astype(jnp.bfloat16)
    return np.concatenate([high, low], 0)


def form_beams(w, head, v, flags):
    slots = 4
    vmem = pl.BlockSpec(memory_space=pltpu.VMEM)
    return pl.pallas_call(
        beams_kernel,
        in_specs=[pl.BlockSpec(memory_space=pltpu.HBM), vmem, vmem, vmem, vmem],
        out_specs=vmem,
        out_shape=jax.ShapeDtypeStruct((2 * BEAMS, TIME), BF16),
        scratch_shapes=[
            pltpu.VMEM((slots, 2, ROWS, FEEDS), BF16),
            pltpu.SemaphoreType.DMA((slots,)),
            pltpu.VMEM((2, ROWS, 2 * TIME), F32),
            pltpu.VMEM((2 * BEAMS, TIME), F32),
            pltpu.VMEM((2 * BEAMS // ROWS, 8, TIME), F32),
            pltpu.VMEM((2 * BEAMS, TIME), F32),
        ],
        compiler_params=pltpu.CompilerParams(vmem_limit_bytes=32 * 2**20),
        name="beams",
    )(pltpu.with_memory_space_constraint(w, pltpu.HBM), head, v, jnp.asarray(dft_table()), flags)


def finish_kernel(in_ref, power_ref, sums_ref):
    def gather_from(r):
        combo = (r >> 6) * 8 + (r & 7)
        eighth = (r >> 3) & 7
        return (eighth >> 1) * 64 + (combo >> 1) * 4 + (eighth & 1) * 2 + (combo & 1)

    def scatter_from(r):
        combo = r >> 3
        return (combo >> 3) * 64 + (r & 7) * 8 + (combo & 7)

    first, second = onehot(256, gather_from), onehot(256, scatter_from)
    lane = lax.broadcasted_iota(jnp.int32, (8, TIME), 1)
    for q in range(8):
        x = jnp.dot(first, in_ref[q * 256 : (q + 1) * 256, :], preferred_element_type=F32)
        blocks = []
        for group in range(4):
            tiles = [x[group * 64 + i * 8 : group * 64 + i * 8 + 8, :] for i in range(8)]
            for bit in (1, 2, 4):
                upper = (lane & (16 * bit)) != 0
                for i in range(8):
                    if i & bit == 0:
                        low, high = tiles[i], tiles[i | bit]
                        if bit == 4:
                            moved = pltpu.roll(jnp.where(upper, low, high), 64, 1)
                            tiles[i] = jnp.where(upper, moved, low)
                            tiles[i | bit] = jnp.where(upper, high, moved)
                            continue
                        tiles[i] = jnp.where(upper, pltpu.roll(high, 16 * bit, 1), low)
                        tiles[i | bit] = jnp.where(upper, high, pltpu.roll(low, TIME - 16 * bit, 1))
            total = sum(tiles[1:], tiles[0])
            squares = sum([t * t for t in tiles[1:]], tiles[0] * tiles[0])
            for member in range(4):
                gy = group * 4 + member
                at = (gy * 8 + q) * TIME
                sums_ref[0, :, at : at + TIME] = total[2 * member : 2 * member + 2, :]
                sums_ref[1, :, at : at + TIME] = squares[2 * member : 2 * member + 2, :]
            blocks += tiles
        y = jnp.concatenate(blocks, 0).astype(BF16)
        z = jnp.dot(second, y, preferred_element_type=F32).astype(BF16)
        for gy in range(16):
            at = (gy * 8 + q) * TIME
            for beam in range(2):
                row = gy * 16 + beam * 8
                power_ref[beam, :, at : at + TIME] = z[row : row + 8, :]


def finish(received):
    freqs = 512 * 2 * UPCHAN
    return pl.pallas_call(
        finish_kernel,
        out_shape=(
            jax.ShapeDtypeStruct((2, TOUT, freqs), BF16),
            jax.ShapeDtypeStruct((2, 2, freqs), F32),
        ),
        compiler_params=pltpu.CompilerParams(vmem_limit_bytes=24 * 2**20),
        name="finish",
    )(received)


def per_device(voltages, beam_grid, feed_pos, rfi_mask):
    inputs = lax.axis_size("gx")
    chan_dev = voltages.shape[2]
    local_chans = chan_dev // inputs
    sent = regroup(voltages)
    piece = lax.all_to_all(sent, "gx", split_axis=0, concat_axis=0, tiled=True)
    w, head = weights(beam_grid, feed_pos, local_chans)
    flags = rfi_mask.reshape(TOUT, local_chans, UPCHAN).transpose(1, 0, 2).astype(F32)
    piece = piece.reshape(inputs, local_chans, voltages.shape[1], 2 * TIME)
    power = form_beams(w, head, piece, flags.reshape(local_chans, TIME))
    power = power.reshape(512, 4, TIME)
    power = lax.all_to_all(power, ("gx", "gy"), split_axis=0, concat_axis=0, tiled=True)
    return finish(power.reshape(2048, TIME))


def solution(mesh):
    in_specs = (P(None, "gx", "gy", None), P(), P(), P(None, ("gy", "gx")))
    out_specs = (P(("gx", "gy"), None, None), P(None, ("gx", "gy"), None))
    return jax.shard_map(
        per_device, mesh=mesh, in_specs=in_specs, out_specs=out_specs, check_vma=False
    )
```

```python
import functools
import math

import jax
import jax.numpy as jnp
import numpy as np
from jax import lax
from jax.experimental import pallas as pl
from jax.experimental.pallas import tpu as pltpu
from jax.sharding import PartitionSpec as P

FEEDS = 2048
BEAMS = 1024
UPCHAN = 16
TOUT = 8
TIME = 128
ROWS = 256
F32 = jnp.float32
BF16 = jnp.bfloat16


def fit(values, degree):
    cheb = np.polynomial.Chebyshev.interpolate(values, degree, domain=[0.0, 0.25])
    return [float(c) for c in cheb.convert(kind=np.polynomial.Polynomial).coef]


COS = fit(lambda u: np.cos(2 * np.pi * np.sqrt(u)), 6)
SIN = fit(lambda u: 2 * np.pi * np.sinc(2 * np.sqrt(u)), 6)


def onehot(size, source_of):
    row = lax.broadcasted_iota(jnp.int32, (size, size), 0)
    col = lax.broadcasted_iota(jnp.int32, (size, size), 1)
    return (col == source_of(row)).astype(F32).astype(BF16)


def regroup_kernel(v_ref, out_ref, in_buf, out_buf, in_sem, out_sem):
    parts, feeds, chans, time = v_ref.shape
    pieces = [(part, f) for f in range(0, feeds, 16) for part in range(parts)]

    def fetch(n):
        at = (pieces[n][0], pl.ds(pieces[n][1], 16))
        return pltpu.make_async_copy(v_ref.at[at], in_buf.at[at], in_sem.at[n])

    def store(n):
        at = (slice(None), pl.ds(n * 16, 16))
        return pltpu.make_async_copy(out_buf.at[at], out_ref.at[at], out_sem.at[n])

    for n in range(len(pieces)):
        fetch(n).start()
    for n, (part, f) in enumerate(pieces):
        fetch(n).wait()
        for c in range(0, chans, 16):
            tile = jnp.swapaxes(in_buf[part, f : f + 16, c : c + 16], 0, 1)
            out_buf[c : c + 16, f : f + 16, part * time : (part + 1) * time] = tile
        if part == parts - 1:
            store(f // 16).start()
    for n in range(feeds // 16):
        store(n).wait()


def regroup(v):
    parts, feeds, chans, time = v.shape
    shape = (chans, feeds, parts * time)
    return pl.pallas_call(
        regroup_kernel,
        in_specs=[pl.BlockSpec(memory_space=pltpu.HBM)],
        out_specs=pl.BlockSpec(memory_space=pltpu.HBM),
        out_shape=pltpu.HBM(shape, BF16),
        scratch_shapes=[
            pltpu.VMEM(v.shape, BF16),
            pltpu.VMEM(shape, BF16),
            pltpu.SemaphoreType.DMA((parts * feeds // 16,)),
            pltpu.SemaphoreType.DMA((feeds // 16,)),
        ],
        compiler_params=pltpu.CompilerParams(vmem_limit_bytes=16 * 2**20),
        name="regroup",
    )(pltpu.with_memory_space_constraint(v, pltpu.HBM))


def weights_kernel(local_chans, beam_ref, feed_ref, out_ref, head_ref, turns_ref):
    device = lax.axis_index("gy") * lax.axis_size("gx") + lax.axis_index("gx")
    factor = (device * local_chans + pl.program_id(0) + 400) % 4096
    bm = beam_ref.shape[1]

    def rows_of(ref):
        row = lax.broadcasted_iota(jnp.int32, (16, ref.shape[1]), 0)
        return row, jnp.where(row < 2, ref[0:1, :], ref[1:2, :])

    row, grid = rows_of(beam_ref)
    part = (grid * factor) & 4095
    left = jnp.where((row & 1) == 0, part & 4032, part & 63)
    left = jnp.where(row < 4, left, 0).astype(F32).astype(BF16)
    right = rows_of(feed_ref)[1].astype(F32).astype(BF16)
    turns_ref[...] = lax.dot_general(
        left, right, (((0,), (0,)), ((), ())), preferred_element_type=F32
    )
    scale = 1.0 / math.sqrt(FEEDS)
    width = 512

    def chunk(i, carry):
        r0 = pl.multiple_of(i * 16, 16)
        for c0 in range(0, FEEDS, width):
            t = turns_ref[pl.ds(r0, 16), c0 : c0 + width] * (1.0 / 4096.0)
            r = t - jnp.round(t)
            u = r * r
            c = COS[-1] * scale
            for coef in COS[-2::-1]:
                c = c * u + coef * scale
            s = -SIN[-1] * scale
            for coef in SIN[-2::-1]:
                s = s * u - coef * scale
            out_ref[0, 0, 0, pl.ds(r0, 16), c0 : c0 + width] = c.astype(BF16)
            out_ref[0, 0, 1, pl.ds(r0, 16), c0 : c0 + width] = (s * r).astype(BF16)
        return carry

    lax.fori_loop(0, bm // 16, chunk, 0)

    @pl.when((pl.program_id(0) == 0) & (pl.program_id(1) == 0))
    def _():
        head_ref[...] = out_ref[0, 0]


def weights(beam_grid, feed_pos, local_chans):
    bm = 128
    per = ROWS // bm
    return pl.pallas_call(
        functools.partial(weights_kernel, local_chans),
        grid=(local_chans, BEAMS // bm),
        in_specs=[
            pl.BlockSpec((2, bm), lambda c, m: (0, m)),
            pl.BlockSpec((2, FEEDS), lambda c, m: (0, 0)),
        ],
        out_specs=(
            pl.BlockSpec((1, 1, 2, bm, FEEDS), lambda c, m: (c, m // per, 0, m % per, 0)),
            pl.BlockSpec((2, bm, FEEDS), lambda c, m: (0, 0, 0)),
        ),
        out_shape=(
            pltpu.HBM((local_chans, BEAMS // ROWS, 2, ROWS, FEEDS), BF16),
            jax.ShapeDtypeStruct((2, bm, FEEDS), BF16),
        ),
        scratch_shapes=[pltpu.VMEM((bm, FEEDS), F32)],
        compiler_params=pltpu.CompilerParams(vmem_limit_bytes=24 * 2**20),
        cost_estimate=pl.CostEstimate(
            flops=30 * local_chans * BEAMS * FEEDS * 20,
            bytes_accessed=local_chans * BEAMS * FEEDS * 4,
            transcendentals=0,
        ),
        name="weights",
    )(beam_grid.T, feed_pos.T)


def split(x):
    high = x.astype(BF16)
    return high, (x - high.astype(F32)).astype(BF16)


def beams_kernel(
    w_hbm, head_ref, v_ref, table_ref, flags_ref, out_ref, w_buf, sem, beam_ref, inten_ref, sum_ref, rows_ref
):
    slots = w_buf.shape[0]
    steps = BEAMS // ROWS
    size = 2 * TIME

    def fetch(i):
        return pltpu.make_async_copy(w_hbm.at[i // steps, i % steps], w_buf.at[i % slots], sem.at[i % slots])

    kept = head_ref.shape[1]
    for part in range(2):
        rest = pl.ds(kept, ROWS - kept)
        pltpu.make_async_copy(w_hbm.at[0, 0, part, rest], w_buf.at[0, part, rest], sem.at[0]).start()
        first = w_buf.at[0, part, pl.ds(0, kept)]
        pltpu.make_async_copy(head_ref.at[part], first, sem.at[0]).start()
    for i in range(1, slots):
        fetch(i).start()
    beam_ref[1] = jnp.zeros_like(beam_ref[1])
    sum_ref[...] = jnp.zeros_like(sum_ref)

    def detect(i):
        high, low = split(beam_ref[i % 2])
        fine = (
            jnp.dot(high, table_ref[:size], preferred_element_type=F32)
            + jnp.dot(high, table_ref[size:], preferred_element_type=F32)
            + jnp.dot(low, table_ref[:size], preferred_element_type=F32)
        )
        real, imag = fine[:, :TIME], fine[:, TIME:]
        intensity = real * real + imag * imag
        inten_ref[pl.ds(pl.multiple_of(i * ROWS, ROWS), ROWS), :] = intensity
        sum_ref[i] = jnp.sum(intensity.reshape(ROWS // 8, 8, TIME), axis=0)

    def normalize(chan):
        total = jnp.sum(sum_ref[chan * steps : (chan + 1) * steps], axis=0)
        total = jnp.broadcast_to(jnp.sum(total, axis=0, keepdims=True), (8, TIME))
        for shift in (64, 32, 16):
            total = total + pltpu.roll(total, shift, 1)
        bandpass = total[0:1] * (1.0 / (BEAMS * TOUT)) + 1e-06
        scale = flags_ref[chan : chan + 1, :] / bandpass

        def move(j, carry):
            for beam in range(2):
                x = inten_ref[pl.ds(chan * BEAMS + j * 128 + beam, 64, stride=2), :]
                rows_ref[pl.ds(j * 256 + 2 * chan + beam, 64, stride=4), :] = x * scale
            if chan == 1:
                rows = pl.ds(pl.multiple_of(j * 256, 256), 256)
                out_ref[rows, :] = rows_ref[rows, :].astype(BF16)
            return carry

        lax.fori_loop(0, BEAMS // 128, move, 0, unroll=True)

    def body(i, carry):
        fetch(i).wait()
        rhs = v_ref[:, i // steps].reshape(FEEDS, size)
        part = jnp.dot(w_buf[i % slots].reshape(2 * ROWS, FEEDS), rhs, preferred_element_type=F32)
        detect(jnp.maximum(i - 1, 0))
        beam_ref[i % 2, :, :TIME] = part[:ROWS, :TIME] - part[ROWS:, TIME:]
        beam_ref[i % 2, :, TIME:] = part[:ROWS, TIME:] + part[ROWS:, :TIME]

        @pl.when(i + slots < 2 * steps)
        def _():
            fetch(i + slots).start()

        @pl.when(i == steps)
        def _():
            normalize(0)

        return carry

    lax.fori_loop(0, 2 * steps, body, 0)
    detect(2 * steps - 1)
    normalize(1)


def dft_table():
    n = np.arange(TIME)
    same = n[:, None] // UPCHAN == n[None, :] // UPCHAN
    angle = 2 * np.pi * ((n[:, None] * n[None, :]) % UPCHAN) / UPCHAN
    cos, sin = np.cos(angle) * same / 4.0, np.sin(angle) * same / 4.0
    table = np.block([[cos, -sin], [sin, cos]]).astype(np.float32)
    high = table.astype(jnp.bfloat16)
    low = (table - high.astype(np.float32)).astype(jnp.bfloat16)
    return np.concatenate([high, low], 0)


def form_beams(w, head, v, flags):
    slots = 6
    vmem = pl.BlockSpec(memory_space=pltpu.VMEM)
    return pl.pallas_call(
        beams_kernel,
        in_specs=[pl.BlockSpec(memory_space=pltpu.HBM), vmem, vmem, vmem, vmem],
        out_specs=vmem,
        out_shape=jax.ShapeDtypeStruct((2 * BEAMS, TIME), BF16),
        scratch_shapes=[
            pltpu.VMEM((slots, 2, ROWS, FEEDS), BF16),
            pltpu.SemaphoreType.DMA((slots,)),
            pltpu.VMEM((2, ROWS, 2 * TIME), F32),
            pltpu.VMEM((2 * BEAMS, TIME), F32),
            pltpu.VMEM((2 * BEAMS // ROWS, 8, TIME), F32),
            pltpu.VMEM((2 * BEAMS, TIME), F32),
        ],
        compiler_params=pltpu.CompilerParams(vmem_limit_bytes=32 * 2**20),
        name="beams",
    )(pltpu.with_memory_space_constraint(w, pltpu.HBM), head, v, jnp.asarray(dft_table()), flags)


def finish_kernel(in_ref, power_ref, sums_ref):
    def gather_from(r):
        combo = (r >> 6) * 8 + (r & 7)
        eighth = (r >> 3) & 7
        return (eighth >> 1) * 64 + (combo >> 1) * 4 + (eighth & 1) * 2 + (combo & 1)

    def scatter_from(r):
        combo = r >> 3
        return (combo >> 3) * 64 + (r & 7) * 8 + (combo & 7)

    first, second = onehot(256, gather_from), onehot(256, scatter_from)
    lane = lax.broadcasted_iota(jnp.int32, (8, TIME), 1)
    for q in range(8):
        x = jnp.dot(first, in_ref[q * 256 : (q + 1) * 256, :], preferred_element_type=F32)
        blocks = []
        for group in range(4):
            tiles = [x[group * 64 + i * 8 : group * 64 + i * 8 + 8, :] for i in range(8)]
            for bit in (1, 2, 4):
                upper = (lane & (16 * bit)) != 0
                for i in range(8):
                    if i & bit == 0:
                        low, high = tiles[i], tiles[i | bit]
                        if bit == 4:
                            moved = pltpu.roll(jnp.where(upper, low, high), 64, 1)
                            tiles[i] = jnp.where(upper, moved, low)
                            tiles[i | bit] = jnp.where(upper, high, moved)
                            continue
                        tiles[i] = jnp.where(upper, pltpu.roll(high, 16 * bit, 1), low)
                        tiles[i | bit] = jnp.where(upper, high, pltpu.roll(low, TIME - 16 * bit, 1))
            total = sum(tiles[1:], tiles[0])
            squares = sum([t * t for t in tiles[1:]], tiles[0] * tiles[0])
            for member in range(4):
                gy = group * 4 + member
                at = (gy * 8 + q) * TIME
                sums_ref[0, :, at : at + TIME] = total[2 * member : 2 * member + 2, :]
                sums_ref[1, :, at : at + TIME] = squares[2 * member : 2 * member + 2, :]
            blocks += tiles
        y = jnp.concatenate(blocks, 0).astype(BF16)
        z = jnp.dot(second, y, preferred_element_type=F32).astype(BF16)
        for gy in range(16):
            at = (gy * 8 + q) * TIME
            for beam in range(2):
                row = gy * 16 + beam * 8
                power_ref[beam, :, at : at + TIME] = z[row : row + 8, :]


def finish(received):
    freqs = 512 * 2 * UPCHAN
    return pl.pallas_call(
        finish_kernel,
        out_shape=(
            jax.ShapeDtypeStruct((2, TOUT, freqs), BF16),
            jax.ShapeDtypeStruct((2, 2, freqs), F32),
        ),
        compiler_params=pltpu.CompilerParams(vmem_limit_bytes=24 * 2**20),
        name="finish",
    )(received)


def per_device(voltages, beam_grid, feed_pos, rfi_mask):
    inputs = lax.axis_size("gx")
    chan_dev = voltages.shape[2]
    local_chans = chan_dev // inputs
    sent = regroup(voltages)
    piece = lax.all_to_all(sent, "gx", split_axis=0, concat_axis=0, tiled=True)
    w, head = weights(beam_grid, feed_pos, local_chans)
    flags = rfi_mask.reshape(TOUT, local_chans, UPCHAN).transpose(1, 0, 2).astype(F32)
    piece = piece.reshape(inputs, local_chans, voltages.shape[1], 2 * TIME)
    power = form_beams(w, head, piece, flags.reshape(local_chans, TIME))
    power = power.reshape(512, 4, TIME)
    power = lax.all_to_all(power, ("gx", "gy"), split_axis=0, concat_axis=0, tiled=True)
    return finish(power.reshape(2048, TIME))


def solution(mesh):
    in_specs = (P(None, "gx", "gy", None), P(), P(), P(None, ("gy", "gx")))
    out_specs = (P(("gx", "gy"), None, None), P(None, ("gx", "gy"), None))
    return jax.shard_map(
        per_device, mesh=mesh, in_specs=in_specs, out_specs=out_specs, check_vma=False
    )
```
